32 devices in a mesh: leaf: 32 (over z, y, x, core).
Axes of the slice: x: 2, y: 2, z: 4, core: 2. Of those that a mesh axis runs over, the one named last changes fastest.
Arguments:
- probes: float32 [32768, 1024], P('leaf'), may hold values from -6 to 6
- leaf_basis: float32 [64, 512, 64], P('leaf'), may hold values from -0.25 to 0.25
- leaf_transfer: float32 [64, 64, 64], P('leaf'), may hold values from -0.75 to 0.75
- cluster_transfer: float32 [16, 64, 64], replicated, may hold values from -0.75 to 0.75
- couple_one: float32 [128, 64, 64], P('leaf'), may hold values from -0.75 to 0.75
- pairs_one: int32 [128], P('leaf'), may hold values from 0 to 15, as said below
- count_one: int32 [16], replicated, may hold values from 0 to 8
- couple_two: float32 [32, 64, 64], P('leaf'), may hold values from -0.75 to 0.75
- pairs_two: int32 [32], P('leaf'), may hold values from 0 to 3, as said below
- count_two: int32 [4], replicated, may hold values from 0 to 2
- near_blocks: float32 [64, 3, 512, 512], P('leaf'), may hold values from -0.15625 to 0.15625
- near_list: int32 [64, 3], P('leaf'), may hold values from 0 to 63, as said below
Outputs:
- kernel_times: float32 [32768, 1024], P('leaf')
The draws below stay inside these ranges and needn't reach their ends.
Inputs may be any that keep to these rules, and one draw needn't show every extreme that they name: `pairs_one`: for slots k < count_one[c], the partners of cluster c are distinct clusters j with |j - c| >= 2 and |j // 4 - c // 4| <= 1; the other slots hold c itself. `pairs_two`: for slots k < count_two[q], the partners of cluster q are distinct clusters j with |j - q| >= 2 and |j // 4 - q // 4| <= 1; the other slots hold q itself. near_list[i, 0] is i, and every entry of row i lies within i - 2 to i + 2.
All inputs are finite; a program needn't handle non-finite values.
Results may differ from the reference program's by a relative error of at most 0.000086.
Values sent between devices are 32-bit elements; how exact they have to be, the bound alone decides.
A program may use at most 128 MiB of HBM per device.

```python
import jax
import jax.numpy as jnp
from jax import lax

LEAF = 512
RANK = 64
PROBES = 1024
NEAR = 3
COUPLE_SLOTS = 8
LEAVES = 64
POINTS = 32768
CLUSTERS_ONE = 16
CLUSTERS_TWO = 4


offset_table = (-7, -6, -5, -4, -3, -2, 2, 3, 4, 5, 6, 7)


near_table = (-2, -1, 1, 2)


def partner_table(key, clusters):
    centers = jnp.arange(clusters, dtype=jnp.int32)[:, None]
    offsets = jnp.array(offset_table, jnp.int32)[None, :]
    candidate = centers + offsets
    usable = (candidate >= 0) & (candidate < clusters) & (jnp.abs(jnp.floor_divide(candidate, 4) - centers // 4) <= 1)
    scores = jax.random.randint(jax.random.fold_in(key, 1), (clusters, 12), 0, 1024) * 16 + jnp.arange(12, dtype=jnp.int32)[None, :]
    scores = jnp.where(usable, scores, scores + 65536)
    ranking = jnp.argsort(scores, axis=1, stable=True)
    chosen = jnp.take_along_axis(candidate, ranking, axis=1)[:, :COUPLE_SLOTS]
    usable_count = jnp.minimum(jnp.sum(usable.astype(jnp.int32), axis=1), COUPLE_SLOTS)
    tie_break = jax.random.randint(jax.random.fold_in(key, 4), (clusters,), 0, 1024)
    busiest = jnp.argmax(usable_count * 1024 + tie_break).astype(jnp.int32)
    loaded = jax.random.randint(jax.random.fold_in(key, 2), (clusters,), 0, 4) == 0
    loaded = loaded | (jnp.arange(clusters, dtype=jnp.int32) == busiest)
    spread = jax.random.randint(jax.random.fold_in(key, 3), (clusters,), 0, 1 << 20) % (usable_count + 1)
    counts = jnp.where(loaded, usable_count, spread)
    slot_index = jnp.arange(COUPLE_SLOTS, dtype=jnp.int32)[None, :]
    partner_ids = jnp.where(slot_index < counts[:, None], chosen, centers)
    return (partner_ids.reshape(-1).astype(jnp.int32), counts.astype(jnp.int32))


def draw_pairs_one(key, part):
    return partner_table(jax.random.fold_in(key, 11), CLUSTERS_ONE)[0]


def draw_count_one(key, part):
    return partner_table(jax.random.fold_in(key, 11), CLUSTERS_ONE)[1]


def draw_pairs_two(key, part):
    return partner_table(jax.random.fold_in(key, 22), CLUSTERS_TWO)[0]


def draw_count_two(key, part):
    return partner_table(jax.random.fold_in(key, 22), CLUSTERS_TWO)[1]


def draw_near_list(key, part):
    leaf_ids = jnp.arange(LEAVES, dtype=jnp.int32)[:, None]
    scores = jax.random.randint(jax.random.fold_in(key, 5), (LEAVES, 4), 0, 1024) * 8 + jnp.arange(4, dtype=jnp.int32)[None, :]
    ranking = jnp.argsort(scores, axis=1, stable=True)[:, :NEAR - 1]
    offsets = jnp.take(jnp.array(near_table, jnp.int32), ranking)
    target = leaf_ids + offsets
    target = jnp.where((target < 0) | (target >= LEAVES), leaf_ids - offsets, target)
    return jnp.concatenate([leaf_ids, target], axis=1).astype(jnp.int32)


def levels(stream_key, dims, cuts, smallest, top_value):
    def one(axis_at, parts):
        steps = jax.random.uniform(jax.random.fold_in(jax.random.fold_in(stream_key, 6), axis_at), (parts,), jnp.float32, smallest / len(cuts), top_value / len(cuts))
        return jnp.repeat(jnp.exp(steps), dims[axis_at] // parts).reshape((-1,) + (1,) * (len(dims) - axis_at - 1))

    factor_of = one(*cuts[0])
    for cut in cuts[1:]:
        factor_of = factor_of * one(*cut)
    return factor_of


def scatter_about(key, shape, scale, bound, shards=(), held_as=jnp.bfloat16):
    factor_of = levels(key, shape, shards, -0.22, 0.18) if shards else 1.0
    entries = jax.random.normal(key, shape, jnp.float32) * scale * factor_of
    return jnp.minimum(jnp.maximum(entries, -bound), bound).astype(held_as)


def setup_inputs(seed: int = 0) -> dict:
    arg_keys = jax.random.split(jax.random.key(seed), 13)
    probes = scatter_about(arg_keys[0], (POINTS, PROBES), 1.0, 6.0, ((0, 32),), jnp.float32)
    leaf_basis = scatter_about(arg_keys[1], (LEAVES, LEAF, RANK), LEAF ** -0.5, 0.25, ((0, 32),), jnp.float32)
    leaf_transfer = scatter_about(arg_keys[2], (LEAVES, RANK, RANK), RANK ** -0.5, 0.75, ((0, 32),), jnp.float32)
    cluster_transfer = scatter_about(arg_keys[3], (CLUSTERS_ONE, RANK, RANK), RANK ** -0.5, 0.75, (), jnp.float32)
    couple_one = scatter_about(arg_keys[4], (CLUSTERS_ONE * COUPLE_SLOTS, RANK, RANK), RANK ** -0.5, 0.75, ((0, 32),), jnp.float32)
    pairs_one = draw_pairs_one(jax.random.fold_in(arg_keys[12], 71), 0)
    count_one = draw_count_one(jax.random.fold_in(arg_keys[12], 71), 0)
    couple_two = scatter_about(arg_keys[7], (CLUSTERS_TWO * COUPLE_SLOTS, RANK, RANK), RANK ** -0.5, 0.75, ((0, 32),), jnp.float32)
    pairs_two = draw_pairs_two(jax.random.fold_in(arg_keys[12], 71), 0)
    count_two = draw_count_two(jax.random.fold_in(arg_keys[12], 71), 0)
    near_blocks = scatter_about(arg_keys[10], (LEAVES, NEAR, LEAF, LEAF), (LEAF * NEAR) ** -0.5, 0.15625, ((0, 32),), jnp.float32)
    near_list = draw_near_list(jax.random.fold_in(arg_keys[12], 71), 0)
    return dict(probes=probes, leaf_basis=leaf_basis, leaf_transfer=leaf_transfer, cluster_transfer=cluster_transfer, couple_one=couple_one, pairs_one=pairs_one, count_one=count_one, couple_two=couple_two, pairs_two=pairs_two, count_two=count_two, near_blocks=near_blocks, near_list=near_list)


def couple_level(coeffs, partner_ids, counts, coupling):
    highest = lax.Precision.HIGHEST
    clusters = counts.shape[0]
    slot_index = jnp.arange(COUPLE_SLOTS, dtype=jnp.int32)[None, :]
    valid = (slot_index < counts[:, None]).astype(jnp.float32).reshape(-1)
    partner = jnp.take(coeffs, partner_ids, axis=0) * valid[:, None, None]
    terms = jnp.einsum("krs,ksp->krp", coupling, partner, precision=highest)
    return terms.reshape(clusters, COUPLE_SLOTS, terms.shape[1], terms.shape[2]).sum(1)


def reference(probes, leaf_basis, leaf_transfer, cluster_transfer, couple_one, pairs_one, count_one, couple_two, pairs_two, count_two, near_blocks, near_list):
    highest = lax.Precision.HIGHEST
    leaf_total, leaf_size, rank_size = leaf_basis.shape
    width = probes.shape[1]
    blocks = probes.reshape(leaf_total, leaf_size, width)
    leaf_coef = jnp.einsum("lnr,lnp->lrp", leaf_basis, blocks, precision=highest)
    coef_one = jnp.einsum("lrs,lrp->lsp", leaf_transfer, leaf_coef, precision=highest)
    coef_one = coef_one.reshape(-1, 4, rank_size, width).sum(1)
    coef_two = jnp.einsum("crs,crp->csp", cluster_transfer, coef_one, precision=highest)
    coef_two = coef_two.reshape(-1, 4, rank_size, width).sum(1)
    far_one = couple_level(coef_one, pairs_one, count_one, couple_one)
    far_two = couple_level(coef_two, pairs_two, count_two, couple_two)
    down_one = far_one + jnp.einsum("crs,csp->crp", cluster_transfer, jnp.repeat(far_two, 4, axis=0), precision=highest)
    child = jnp.einsum("lrs,lsp->lrp", leaf_transfer, jnp.repeat(down_one, 4, axis=0), precision=highest)
    far_rows = jnp.einsum("lnr,lrp->lnp", leaf_basis, child, precision=highest)

    def near_leaf(item):
        leaf_blocks, leaf_ids = item
        rows = jnp.take(blocks, leaf_ids, axis=0)
        return jnp.einsum("mab,mbp->ap", leaf_blocks, rows, precision=highest)

    near_rows = lax.map(near_leaf, (near_blocks, near_list))
    return (far_rows + near_rows).reshape(-1, width)
```

```python
import functools

import jax
import jax.numpy as jnp
from jax import lax
from jax.experimental import pallas as pl
from jax.experimental.pallas import tpu as pltpu
from jax.sharding import PartitionSpec as P

MESH = pl.DeviceIdType.MESH
GROUP = 4
LANES = 128
partner_offsets = (-7, -6, -5, -4, -3, -2, 2, 3, 4, 5, 6, 7)


def split(x):
    high = x.astype(jnp.bfloat16)
    low = (x - high.astype(jnp.float32)).astype(jnp.bfloat16)
    return high, low


def dot_split(a, b):
    one = functools.partial(jnp.dot, preferred_element_type=jnp.float32)
    return one(a[0], b[0]) + (one(a[0], b[1]) + one(a[1], b[0]))


def dot(a, b):
    return dot_split(split(a), split(b))


def kernel(
    devices,
    offsets,
    probes,
    basis,
    transfer,
    cluster,
    cone,
    pone,
    none,
    ctwo,
    ptwo,
    ntwo,
    near,
    nlist,
    out,
    *scratch,
):
    chunks = len(scratch) - 19
    bufs = scratch[:chunks]
    (near_f, near_h, near_l, total, part, half, share, coef, own_two, two, packed, down, dn, lift,
     send, recv, halo_send, halo_recv, near_sem) = scratch[chunks:]
    leaves, size, rank = basis.shape
    wide = bufs[0].shape[2]
    per_chunk = wide // LANES
    me = lax.axis_index("leaf")
    plane_size = GROUP * 2
    planes = devices // plane_size
    q = lax.div(me, plane_size)
    r = lax.rem(me, plane_size)
    core = lax.rem(r, 2)
    c4 = lax.div(r, 2)
    mate = me + 1 - 2 * core
    beside = me - 1 + 2 * core
    has_beside = (beside >= 0) & (beside < devices)

    def chip(t):
        return q * plane_size + t * 2 + core

    def xor(value, bits):
        result = value
        for bit in (1, 2):
            if bits & bit:
                result = result + bit - 2 * bit * lax.rem(lax.div(value, bit), 2)
        return result

    def reaches(o):
        other = q + o
        apart = lax.div(other + 8, GROUP) - lax.div(q + 8, GROUP)
        return (other >= 0) & (other < planes) & (apart <= 1) & (apart >= -1)

    def remote(src, dst, ss, rs, device):
        return pltpu.make_async_remote_copy(
            src_ref=src, dst_ref=dst, send_sem=ss, recv_sem=rs,
            device_id=(device,), device_id_type=MESH,
        )

    def go(index, src, dst, device):
        return remote(src, dst, send.at[index], recv.at[index], device)

    barrier = pltpu.get_barrier_semaphore()

    def greet(device):
        pl.semaphore_signal(barrier, inc=1, device_id=(device,), device_id_type=MESH)

    greet(mate)
    for s in (1, 2, 3):
        greet(chip(xor(c4, s)))
    maybe = [(has_beside, beside), (q > 0, me - plane_size), (q < planes - 1, me + plane_size)]
    maybe += [(reaches(o), me + o * plane_size) for o in offsets]
    expected = jnp.int32(4)
    for there, device in maybe:
        pl.when(there)(functools.partial(greet, device))
        expected = expected + jnp.where(there, 1, 0)
    pl.semaphore_wait(barrier, expected)

    def halo(k, far):
        src = probes.at[:, :, pl.ds(k * wide, wide)]
        if far:
            dst = bufs[k].at[pl.ds((1 - core) * 2 * leaves, leaves)]
            return remote(src, dst, halo_send.at[0, k], halo_recv.at[0, k], beside)
        dst = bufs[k].at[pl.ds(core * 2 * leaves, leaves)]
        return remote(src, dst, halo_send.at[1, k], halo_recv.at[1, k], mate)

    own_copies = [
        pltpu.make_async_copy(
            probes.at[:, :, pl.ds(k * wide, wide)],
            bufs[k].at[pl.ds(leaves, leaves)],
            near_sem.at[k],
        )
        for k in range(chunks)
    ]
    near_copy = pltpu.make_async_copy(near, near_f, near_sem.at[chunks])
    for copy in own_copies:
        copy.start()

    for k in range(chunks):
        pl.when(has_beside)(halo(k, True).start)
    for k in range(chunks):
        halo(k, False).start()

    near_copy.start()

    slot = core * GROUP + c4
    slots = cone.shape[0]
    for s in range(slots // 2):
        packed[slot, pl.ds(s * rank, rank), :] = jnp.concatenate(
            [cone[2 * s], cone[2 * s + 1]], axis=1
        )
    packed[slot, pl.ds(slots // 2 * rank, rank), :] = jnp.concatenate([ctwo[0], ctwo[0]], axis=1)
    mine = q * GROUP + c4
    ids = [
        jnp.where(core * slots + k < none[mine], pone[k], -1) for k in range(slots)
    ]
    ids.append(jnp.where(r < ntwo[q], ptwo[0], -1))
    row = lax.broadcasted_iota(jnp.int32, (8, LANES), 0)
    table = jnp.full((8, LANES), -1, jnp.int32)
    for k, value in enumerate(ids):
        table = jnp.where(row == k, value, table)
    id_row = slots // 2 * rank + rank
    packed[slot, pl.ds(id_row, 8), :] = table.astype(jnp.float32)
    bit_x, bit_y = lax.rem(c4, 2), lax.div(c4, 2)
    pack_x = go(6, packed.at[pl.ds(slot, 1)], packed.at[pl.ds(slot, 1)], chip(xor(c4, 1)))
    pair = core * GROUP + bit_y * 2
    pack_y = go(7, packed.at[pl.ds(pair, 2)], packed.at[pl.ds(pair, 2)], chip(xor(c4, 2)))
    quad = core * GROUP
    pack_c = go(8, packed.at[pl.ds(quad, 4)], packed.at[pl.ds(quad, 4)], mate)
    pack_x.start()

    for l in range(leaves):
        lift[l] = dot(basis[l], transfer[l])
    lifts = [split(lift[l].T) for l in range(leaves)]
    for k in range(chunks):
        own_copies[k].wait()
        value = sum(
            dot_split(lifts[l], split(bufs[k][leaves + l]))
            for l in range(leaves)
        )
        for g in range(per_chunk):
            part[k * per_chunk + g] = value[:, g * LANES:(g + 1) * LANES]
    halve = go(0, part.at[pl.ds((1 - core) * GROUP, GROUP)], half, mate)
    halve.start()
    pack_x.wait_recv()
    pack_y.start()
    halve.wait_recv()
    for t in range(GROUP):
        share[t] = part[core * GROUP + t] + half[t]
    spread = [
        go(s, share.at[xor(c4, s)], coef.at[GROUP + c4], chip(xor(c4, s))) for s in (1, 2, 3)
    ]
    for copy in spread:
        copy.start()
    coef[GROUP + c4] = share[c4]
    pack_y.wait_recv()
    pack_c.start()

    def near_split(index, _):
        l, m = lax.div(index, near.shape[1]), lax.rem(index, near.shape[1])
        near_h[l, m], near_l[l, m] = split(near_f[l, m])
        return _

    near_copy.wait()
    lax.fori_loop(0, leaves * near.shape[1], near_split, 0)

    for copy in spread:
        copy.wait_recv()
    up = go(4, coef.at[pl.ds(GROUP, GROUP)], coef.at[pl.ds(0, GROUP)], me + plane_size)
    lower = go(5, coef.at[pl.ds(GROUP, GROUP)], coef.at[pl.ds(2 * GROUP, GROUP)], me - plane_size)
    pl.when(q < planes - 1)(up.start)
    pl.when(q > 0)(lower.start)
    own_two[...] = sum(
        dot(cluster[q * GROUP + j].T, coef[GROUP + j]) for j in range(GROUP)
    )
    two_copies = []
    for i, o in enumerate(offsets):
        copy = go(13 + i, own_two, two.at[offsets.index(-o)], me + o * plane_size)
        two_copies.append((o, copy))
        pl.when(reaches(o))(copy.start)

    def own_near(l, _):
        at = pl.ds(pl.multiple_of(l * size, size), size)
        for k in range(chunks):
            x = bufs[k][leaves + l]
            total[at, k * wide:(k + 1) * wide] = dot_split((near_h[l, 0], near_l[l, 0]), split(x))
        return _

    lax.fori_loop(0, leaves, own_near, 0)

    pl.when(q > 0)(up.wait_recv)
    pl.when(q < planes - 1)(lower.wait_recv)
    for o, copy in two_copies:
        pl.when(reaches(-o))(copy.wait_recv)
    pack_c.wait_recv()

    zero = jnp.zeros((rank, LANES), jnp.float32)

    def chosen(at, k, options):
        picked = zero
        label = packed[at, pl.ds(id_row + k, 1), :]
        for number, value in options:
            picked = jnp.where(label == number.astype(jnp.float32), value, picked)
        return picked

    far_two = zero
    for at in range(plane_size):
        options = [(q + o, two[i]) for i, o in enumerate(offsets)]
        far_two += dot(
            packed[at, pl.ds(slots // 2 * rank, rank), :][:, :rank], chosen(at, slots, options)
        )

    far_two_split = split(far_two)

    def cluster_far(j, _):
        value = dot_split(split(cluster[q * GROUP + j]), far_two_split)
        options = [((q - 1) * GROUP + i, coef[i]) for i in range(3 * GROUP)]
        for k in range(2):
            at = k * GROUP + j
            for s in range(slots // 2):
                partner = jnp.concatenate(
                    [chosen(at, 2 * s, options), chosen(at, 2 * s + 1, options)], axis=0
                )
                value += dot(packed[at, pl.ds(s * rank, rank), :], partner)
        down[j] = value
        return _

    lax.fori_loop(0, GROUP, cluster_far, 0)
    mine_at = core * GROUP + c4
    back = [
        go(8 + s, down.at[xor(c4, s)], dn.at[mine_at], chip(xor(c4, s))) for s in (1, 2, 3)
    ]
    for copy in back:
        copy.start()
    dn[mine_at] = down[c4]
    for copy in back:
        copy.wait_recv()
    join = go(12, dn.at[pl.ds(quad, 4)], dn.at[pl.ds(quad, 4)], mate)
    join.start()
    join.wait_recv()

    def far_rows(l, _):
        at = pl.ds(pl.multiple_of(l * size, size), size)
        tall = split(lift[l])
        for k in range(chunks):
            value = jnp.concatenate(
                [dn[k * per_chunk + g] for g in range(per_chunk)], axis=1
            )
            total[at, k * wide:(k + 1) * wide] += dot_split(tall, split(value))
        return _

    lax.fori_loop(0, leaves, far_rows, 0)

    results = []
    for k in range(chunks):
        halo(k, False).wait_recv()
        pl.when(has_beside)(halo(k, True).wait_recv)

        def other_near(l, _, k=k):
            at = pl.ds(pl.multiple_of(l * size, size), size)
            value = total[at, k * wide:(k + 1) * wide]
            for m in range(1, near.shape[1]):
                index = nlist[l, m] - (me - 1) * leaves
                index = jnp.maximum(0, jnp.minimum(index, 3 * leaves - 1))
                value += dot_split((near_h[l, m], near_l[l, m]), split(bufs[k][index]))
            total[at, k * wide:(k + 1) * wide] = value
            return _

        lax.fori_loop(0, leaves, other_near, 0)
        copy = pltpu.make_async_copy(
            total.at[:, pl.ds(k * wide, wide)],
            out.at[:, pl.ds(k * wide, wide)],
            near_sem.at[k],
        )
        copy.start()
        results.append(copy)

    for copy in [halve, pack_x, pack_y, pack_c, join] + spread + back:
        copy.wait_send()
    pl.when(q < planes - 1)(up.wait_send)
    pl.when(q > 0)(lower.wait_send)
    for o, copy in two_copies:
        pl.when(reaches(o))(copy.wait_send)
    for k in range(chunks):
        halo(k, False).wait_send()
        pl.when(has_beside)(halo(k, True).wait_send)
    for copy in results:
        copy.wait()


def body(devices, *args):
    probes, basis, near = args[0], args[1], args[10]
    slots = args[4].shape[0]
    leaves, size, rank = basis.shape
    rows, width = probes.shape
    planes = devices // (2 * GROUP)
    offsets = tuple(o for o in partner_offsets if abs(o) < planes)
    chunks = 4
    groups = width // LANES
    wide = width // chunks
    assert leaves == 2 and groups == 2 * GROUP and 2 * rank == LANES
    vmem = pl.BlockSpec(memory_space=pltpu.VMEM)
    smem = pl.BlockSpec(memory_space=pltpu.SMEM)
    anywhere = pl.BlockSpec(memory_space=pl.ANY)
    f32, bf16 = jnp.float32, jnp.bfloat16
    small = lambda n: pltpu.VMEM((n, rank, LANES), f32)
    dma = pltpu.SemaphoreType.DMA
    flops = 2 * (near.size + 2 * basis.size) * width
    return pl.pallas_call(
        functools.partial(kernel, devices, offsets),
        out_shape=jax.ShapeDtypeStruct((rows, width), f32),
        in_specs=[anywhere, vmem, vmem, vmem, vmem, smem, smem, vmem, smem, smem, anywhere, smem],
        out_specs=anywhere,
        scratch_shapes=[pltpu.VMEM((3 * leaves, size, wide), f32)] * chunks
        + [
            pltpu.VMEM(near.shape, f32),
            pltpu.VMEM(near.shape, bf16),
            pltpu.VMEM(near.shape, bf16),
            pltpu.VMEM((rows, width), f32),
            small(groups),
            small(GROUP),
            small(GROUP),
            small(3 * GROUP),
            pltpu.VMEM((rank, LANES), f32),
            small(max(1, len(offsets))),
            pltpu.VMEM((2 * GROUP, (slots // 2 + 1) * rank + 8, LANES), f32),
            small(GROUP),
            small(groups),
            pltpu.VMEM((leaves, size, rank), f32),
            dma((13 + len(offsets),)),
            dma((13 + len(offsets),)),
            dma((2, chunks)),
            dma((2, chunks)),
            dma((chunks + 1,)),
        ],
        compiler_params=pltpu.CompilerParams(
            collective_id=0, has_side_effects=True, vmem_limit_bytes=52 * 1024 * 1024
        ),
        cost_estimate=pl.CostEstimate(
            flops=3 * flops, bytes_accessed=4 * (near.size + 4 * probes.size), transcendentals=0
        ),
    )(probes.reshape(leaves, size, width), *args[1:])


def solution(mesh):
    return jax.shard_map(
        functools.partial(body, mesh.shape["leaf"]),
        mesh=mesh,
        in_specs=(
            P("leaf", None),
            P("leaf", None, None),
            P("leaf", None, None),
            P(),
            P("leaf", None, None),
            P("leaf"),
            P(),
            P("leaf", None, None),
            P("leaf"),
            P(),
            P("leaf", None, None, None),
            P("leaf", None),
        ),
        out_specs=P("leaf", None),
        check_vma=False,
    )
```

```python
import functools

import jax
import jax.numpy as jnp
from jax import lax
from jax.experimental import pallas as pl
from jax.experimental.pallas import tpu as pltpu
from jax.sharding import PartitionSpec as P

MESH = pl.DeviceIdType.MESH
GROUP = 4
LANES = 128
partner_offsets = (-7, -6, -5, -4, -3, -2, 2, 3, 4, 5, 6, 7)


def split(x):
    high = x.astype(jnp.bfloat16)
    low = (x - high.astype(jnp.float32)).astype(jnp.bfloat16)
    return high, low


def dot_split(a, b):
    one = functools.partial(jnp.dot, preferred_element_type=jnp.float32)
    return one(a[0], b[0]) + (one(a[0], b[1]) + one(a[1], b[0]))


def dot(a, b):
    return dot_split(split(a), split(b))


def kernel(
    devices,
    offsets,
    probes,
    basis_hbm,
    transfer_hbm,
    cluster_hbm,
    cone_hbm,
    pone_hbm,
    none_hbm,
    ctwo_hbm,
    ptwo,
    ntwo_hbm,
    near,
    nlist_hbm,
    out,
    *scratch,
):
    chunks = len(scratch) - 29
    bufs = scratch[:chunks]
    (basis, transfer, cluster, cone, pone, none, ctwo, ntwo, nlist, small_sem,
     near_f, near_h, near_l, total, part, half, share, coef, own_two, two, packed, down, dn, lift,
     send, recv, halo_send, halo_recv, near_sem) = scratch[chunks:]
    leaves, rank, size = basis.shape
    wide = bufs[0].shape[2]
    per_chunk = wide // LANES
    me = lax.axis_index("leaf")
    plane_size = GROUP * 2
    planes = devices // plane_size
    q = lax.div(me, plane_size)
    r = lax.rem(me, plane_size)
    core = lax.rem(r, 2)
    c4 = lax.div(r, 2)
    mate = me + 1 - 2 * core
    beside = me - 1 + 2 * core
    has_beside = (beside >= 0) & (beside < devices)

    def chip(t):
        return q * plane_size + t * 2 + core

    def xor(value, bits):
        result = value
        for bit in (1, 2):
            if bits & bit:
                result = result + bit - 2 * bit * lax.rem(lax.div(value, bit), 2)
        return result

    def reaches(o):
        other = q + o
        apart = lax.div(other + 8, GROUP) - lax.div(q + 8, GROUP)
        return (other >= 0) & (other < planes) & (apart <= 1) & (apart >= -1)

    def remote(src, dst, ss, rs, device):
        return pltpu.make_async_remote_copy(
            src_ref=src, dst_ref=dst, send_sem=ss, recv_sem=rs,
            device_id=(device,), device_id_type=MESH,
        )

    def go(index, src, dst, device):
        return remote(src, dst, send.at[index], recv.at[index], device)

    own_copies = [
        pltpu.make_async_copy(
            probes.at[:, :, pl.ds(k * wide, wide)],
            bufs[k].at[pl.ds(leaves, leaves)],
            near_sem.at[k],
        )
        for k in range(chunks)
    ]
    near_copy = pltpu.make_async_copy(near, near_f, near_sem.at[chunks])
    plane_clusters = cluster_hbm.at[pl.ds(q * GROUP, GROUP)]
    small_copies = [
        pltpu.make_async_copy(a, b, small_sem.at[i])
        for i, (a, b) in enumerate((
            (basis_hbm, basis), (transfer_hbm, transfer), (cone_hbm, cone), (ctwo_hbm, ctwo),
            (pone_hbm, pone), (none_hbm, none), (ntwo_hbm, ntwo),
            (plane_clusters, cluster), (nlist_hbm, nlist),
        ))
    ]
    for copy in small_copies[:2] + own_copies + small_copies[2:]:
        copy.start()

    barrier = pltpu.get_barrier_semaphore()

    def greet(device):
        pl.semaphore_signal(barrier, inc=1, device_id=(device,), device_id_type=MESH)

    greet(mate)
    for s in (1, 2, 3):
        greet(chip(xor(c4, s)))
    maybe = [(has_beside, beside), (q > 0, me - plane_size), (q < planes - 1, me + plane_size)]
    maybe += [(reaches(o), me + o * plane_size) for o in offsets]
    expected = jnp.int32(4)
    for there, device in maybe:
        pl.when(there)(functools.partial(greet, device))
        expected = expected + jnp.where(there, 1, 0)
    pl.semaphore_wait(barrier, expected)

    def halo(k, far, l=0):
        if far:
            src = probes.at[pl.ds(l, 1), :, pl.ds(k * wide, wide)]
            dst = bufs[k].at[pl.ds((1 - core) * 2 * leaves + l, 1)]
            return remote(src, dst, halo_send.at[l, k], halo_recv.at[l, k], beside)
        src = probes.at[:, :, pl.ds(k * wide, wide)]
        dst = bufs[k].at[pl.ds(core * 2 * leaves, leaves)]
        return remote(src, dst, halo_send.at[leaves, k], halo_recv.at[leaves, k], mate)

    def piece(p):
        pl.when(has_beside)(halo(p // leaves, True, p % leaves).start)

    piece(0)
    piece(1)
    near_copy.start()

    for copy in small_copies[:2]:
        copy.wait()
    flat = [dot(transfer[l].T, basis[l]) for l in range(leaves)]
    lifts = [split(value) for value in flat]
    for l in range(leaves):
        lift[l] = flat[l].T
    for k in range(chunks):
        own_copies[k].wait()
        value = sum(
            dot_split(lifts[l], split(bufs[k][leaves + l]))
            for l in range(leaves)
        )
        for g in range(per_chunk):
            part[k * per_chunk + g] = value[:, g * LANES:(g + 1) * LANES]
    halve = go(0, part.at[pl.ds((1 - core) * GROUP, GROUP)], half, mate)
    halve.start()

    for copy in small_copies[2:]:
        copy.wait()
    slot = core * GROUP + c4
    slots = cone.shape[0]
    for s in range(slots // 2):
        packed[slot, pl.ds(s * rank, rank), :] = jnp.concatenate(
            [cone[2 * s], cone[2 * s + 1]], axis=1
        )
    packed[slot, pl.ds(slots // 2 * rank, rank), :] = jnp.concatenate([ctwo[0], ctwo[0]], axis=1)
    mine = q * GROUP + c4
    ids = [
        jnp.where(core * slots + k < none[mine], pone[k], -1) for k in range(slots)
    ]
    ids.append(jnp.where(r < ntwo[q], ptwo[0], -1))
    row = lax.broadcasted_iota(jnp.int32, (8, LANES), 0)
    table = jnp.full((8, LANES), -1, jnp.int32)
    for k, value in enumerate(ids):
        table = jnp.where(row == k, value, table)
    id_row = slots // 2 * rank + rank
    packed[slot, pl.ds(id_row, 8), :] = table.astype(jnp.float32)
    bit_x, bit_y = lax.rem(c4, 2), lax.div(c4, 2)
    pack_x = go(6, packed.at[pl.ds(slot, 1)], packed.at[pl.ds(slot, 1)], chip(xor(c4, 1)))
    pair = core * GROUP + bit_y * 2
    pack_y = go(7, packed.at[pl.ds(pair, 2)], packed.at[pl.ds(pair, 2)], chip(xor(c4, 2)))
    quad = core * GROUP
    pack_c = go(8, packed.at[pl.ds(quad, 4)], packed.at[pl.ds(quad, 4)], mate)
    pack_x.start()
    halve.wait_recv()
    for t in range(GROUP):
        share[t] = part[core * GROUP + t] + half[t]
    spread = [
        go(s, share.at[xor(c4, s)], coef.at[GROUP + c4], chip(xor(c4, s))) for s in (1, 2, 3)
    ]
    for copy in spread:
        copy.start()
    coef[GROUP + c4] = share[c4]
    piece(2)
    halo(0, False).start()
    pack_x.wait_recv()
    pack_y.start()

    def near_split(index, _):
        l, m = lax.div(index, near.shape[1]), lax.rem(index, near.shape[1])
        near_h[l, m], near_l[l, m] = split(near_f[l, m])
        return _

    near_copy.wait()
    lax.fori_loop(0, leaves * near.shape[1], near_split, 0)

    for copy in spread:
        copy.wait_recv()
    up = go(4, coef.at[pl.ds(GROUP, GROUP)], coef.at[pl.ds(0, GROUP)], me + plane_size)
    lower = go(5, coef.at[pl.ds(GROUP, GROUP)], coef.at[pl.ds(2 * GROUP, GROUP)], me - plane_size)
    pl.when(q < planes - 1)(up.start)
    pl.when(q > 0)(lower.start)
    own_two[...] = sum(
        dot(cluster[j].T, coef[GROUP + j]) for j in range(GROUP)
    )
    two_copies = []
    for i, o in enumerate(offsets):
        copy = go(13 + i, own_two, two.at[offsets.index(-o)], me + o * plane_size)
        two_copies.append((o, copy))
        pl.when(reaches(o))(copy.start)
    piece(3)
    piece(4)
    halo(1, False).start()
    pack_y.wait_recv()
    pack_c.start()

    def own_near(l, _):
        at = pl.ds(pl.multiple_of(l * size, size), size)
        for k in range(chunks):
            x = bufs[k][leaves + l]
            total[at, k * wide:(k + 1) * wide] = dot_split((near_h[l, 0], near_l[l, 0]), split(x))
        return _

    lax.fori_loop(0, leaves, own_near, 0)

    pl.when(q > 0)(up.wait_recv)
    pl.when(q < planes - 1)(lower.wait_recv)
    for o, copy in two_copies:
        pl.when(reaches(-o))(copy.wait_recv)
    pack_c.wait_recv()

    zero = jnp.zeros((rank, LANES), jnp.float32)

    def chosen(at, k, options):
        picked = zero
        label = packed[at, pl.ds(id_row + k, 1), :]
        for number, value in options:
            picked = jnp.where(label == number.astype(jnp.float32), value, picked)
        return picked

    far_two = zero
    for at in range(plane_size):
        options = [(q + o, two[i]) for i, o in enumerate(offsets)]
        far_two += dot(
            packed[at, pl.ds(slots // 2 * rank, rank), :][:, :rank], chosen(at, slots, options)
        )

    far_two_split = split(far_two)

    def cluster_far(j, _):
        value = dot_split(split(cluster[j]), far_two_split)
        options = [((q - 1) * GROUP + i, coef[i]) for i in range(3 * GROUP)]
        for k in range(2):
            at = k * GROUP + j
            for s in range(slots // 2):
                partner = jnp.concatenate(
                    [chosen(at, 2 * s, options), chosen(at, 2 * s + 1, options)], axis=0
                )
                value += dot(packed[at, pl.ds(s * rank, rank), :], partner)
        down[j] = value
        return _

    lax.fori_loop(0, GROUP, cluster_far, 0)
    mine_at = core * GROUP + c4
    back = [
        go(8 + s, down.at[xor(c4, s)], dn.at[mine_at], chip(xor(c4, s))) for s in (1, 2, 3)
    ]
    for copy in back:
        copy.start()
    piece(5)
    halo(2, False).start()
    dn[mine_at] = down[c4]
    for copy in back:
        copy.wait_recv()
    join = go(12, dn.at[pl.ds(quad, 4)], dn.at[pl.ds(quad, 4)], mate)
    join.start()
    for p in range(6, chunks * leaves):
        piece(p)
    for k in range(3, chunks):
        halo(k, False).start()
    join.wait_recv()

    def far_rows(l, _):
        at = pl.ds(pl.multiple_of(l * size, size), size)
        tall = split(lift[l])
        for k in range(chunks):
            value = jnp.concatenate(
                [dn[k * per_chunk + g] for g in range(per_chunk)], axis=1
            )
            total[at, k * wide:(k + 1) * wide] += dot_split(tall, split(value))
        return _

    lax.fori_loop(0, leaves, far_rows, 0)

    results = []
    for k in range(chunks):
        halo(k, False).wait_recv()
        for l in range(leaves):
            pl.when(has_beside)(halo(k, True, l).wait_recv)

        def other_near(l, _, k=k):
            at = pl.ds(pl.multiple_of(l * size, size), size)
            value = total[at, k * wide:(k + 1) * wide]
            for m in range(1, near.shape[1]):
                index = nlist[l, m] - (me - 1) * leaves
                index = jnp.maximum(0, jnp.minimum(index, 3 * leaves - 1))
                value += dot_split((near_h[l, m], near_l[l, m]), split(bufs[k][index]))
            total[at, k * wide:(k + 1) * wide] = value
            return _

        lax.fori_loop(0, leaves, other_near, 0)
        copy = pltpu.make_async_copy(
            total.at[:, pl.ds(k * wide, wide)],
            out.at[:, pl.ds(k * wide, wide)],
            near_sem.at[k],
        )
        copy.start()
        results.append(copy)

    for copy in [halve, pack_x, pack_y, pack_c, join] + spread + back:
        copy.wait_send()
    pl.when(q < planes - 1)(up.wait_send)
    pl.when(q > 0)(lower.wait_send)
    for o, copy in two_copies:
        pl.when(reaches(o))(copy.wait_send)
    for k in range(chunks):
        halo(k, False).wait_send()
        for l in range(leaves):
            pl.when(has_beside)(halo(k, True, l).wait_send)
    for copy in results:
        copy.wait()


def body(devices, *args):
    probes, basis, near = args[0], args[1], args[10]
    slots = args[4].shape[0]
    leaves, size, rank = basis.shape
    rows, width = probes.shape
    planes = devices // (2 * GROUP)
    offsets = tuple(o for o in partner_offsets if abs(o) < planes)
    chunks = 4
    groups = width // LANES
    wide = width // chunks
    assert leaves == 2 and groups == 2 * GROUP and 2 * rank == LANES
    smem = pl.BlockSpec(memory_space=pltpu.SMEM)
    anywhere = pl.BlockSpec(memory_space=pltpu.HBM)
    f32, bf16 = jnp.float32, jnp.bfloat16
    small = lambda n: pltpu.VMEM((n, rank, LANES), f32)
    dma = pltpu.SemaphoreType.DMA
    flops = 2 * (near.size + 2 * basis.size) * width
    return pl.pallas_call(
        functools.partial(kernel, devices, offsets),
        out_shape=jax.ShapeDtypeStruct((rows, width), f32),
        in_specs=[anywhere] * 8 + [smem] + [anywhere] * (len(args) - 9),
        out_specs=anywhere,
        scratch_shapes=[pltpu.VMEM((3 * leaves, size, wide), f32)] * chunks
        + [
            pltpu.VMEM((leaves, rank, size), f32),
            pltpu.VMEM(args[2].shape, f32),
            pltpu.VMEM((GROUP, rank, rank), f32),
            pltpu.VMEM(args[4].shape, f32),
            pltpu.SMEM(args[5].shape, jnp.int32),
            pltpu.SMEM(args[6].shape, jnp.int32),
            pltpu.VMEM(args[7].shape, f32),
            pltpu.SMEM(args[9].shape, jnp.int32),
            pltpu.SMEM(args[11].shape, jnp.int32),
            dma((9,)),
            pltpu.VMEM(near.shape, f32),
            pltpu.VMEM(near.shape, bf16),
            pltpu.VMEM(near.shape, bf16),
            pltpu.VMEM((rows, width), f32),
            small(groups),
            small(GROUP),
            small(GROUP),
            small(3 * GROUP),
            pltpu.VMEM((rank, LANES), f32),
            small(max(1, len(offsets))),
            pltpu.VMEM((2 * GROUP, (slots // 2 + 1) * rank + 8, LANES), f32),
            small(GROUP),
            small(groups),
            pltpu.VMEM((leaves, size, rank), f32),
            dma((13 + len(offsets),)),
            dma((13 + len(offsets),)),
            dma((leaves + 1, chunks)),
            dma((leaves + 1, chunks)),
            dma((chunks + 1,)),
        ],
        compiler_params=pltpu.CompilerParams(
            collective_id=0, has_side_effects=True, vmem_limit_bytes=64 * 1024 * 1024 - 64 * 1024
        ),
        cost_estimate=pl.CostEstimate(
            flops=3 * flops, bytes_accessed=4 * (near.size + 4 * probes.size), transcendentals=0
        ),
    )(probes.reshape(leaves, size, width), jnp.swapaxes(basis, 1, 2), *args[2:])


def solution(mesh):
    return jax.shard_map(
        functools.partial(body, mesh.shape["leaf"]),
        mesh=mesh,
        in_specs=(
            P("leaf", None),
            P("leaf", None, None),
            P("leaf", None, None),
            P(),
            P("leaf", None, None),
            P("leaf"),
            P(),
            P("leaf", None, None),
            P("leaf"),
            P(),
            P("leaf", None, None, None),
            P("leaf", None),
        ),
        out_specs=P("leaf", None),
        check_vma=False,
    )
```

```python
import functools

import jax
import jax.numpy as jnp
from jax import lax
from jax.experimental import pallas as pl
from jax.experimental.pallas import tpu as pltpu
from jax.sharding import PartitionSpec as P

MESH = pl.DeviceIdType.MESH
GROUP = 4
LANES = 128
partner_offsets = (-7, -6, -5, -4, -3, -2, 2, 3, 4, 5, 6, 7)


def split(x):
    high = x.astype(jnp.bfloat16)
    low = (x - high.astype(jnp.float32)).astype(jnp.bfloat16)
    return high, low


def dot_split(a, b):
    one = functools.partial(jnp.dot, preferred_element_type=jnp.float32)
    return one(a[0], b[0]) + (one(a[0], b[1]) + one(a[1], b[0]))


def dot(a, b):
    return dot_split(split(a), split(b))


def kernel(
    devices,
    offsets,
    probes,
    basis_hbm,
    transfer_hbm,
    cluster_hbm,
    cone_hbm,
    pone_hbm,
    none_hbm,
    ctwo_hbm,
    ptwo,
    ntwo_hbm,
    near,
    nlist_hbm,
    out,
    *scratch,
):
    chunks = (len(scratch) - 29) // 2
    bufs, lasts = scratch[:chunks], scratch[chunks:2 * chunks]
    (basis, transfer, cluster, cone, pone, none, ctwo, ntwo, nlist, small_sem,
     near_f, near_h, near_l, total, part, half, share, coef, own_two, two, packed, down, dn, lift,
     send, recv, halo_send, halo_recv, near_sem) = scratch[2 * chunks:]
    leaves, rank, size = basis.shape
    wide = bufs[0].shape[2]
    per_chunk = wide // LANES
    me = lax.axis_index("leaf")
    plane_size = GROUP * 2
    planes = devices // plane_size
    q = lax.div(me, plane_size)
    r = lax.rem(me, plane_size)
    core = lax.rem(r, 2)
    c4 = lax.div(r, 2)
    mate = me + 1 - 2 * core
    beside = me - 1 + 2 * core
    has_beside = (beside >= 0) & (beside < devices)

    def chip(t):
        return q * plane_size + t * 2 + core

    def xor(value, bits):
        result = value
        for bit in (1, 2):
            if bits & bit:
                result = result + bit - 2 * bit * lax.rem(lax.div(value, bit), 2)
        return result

    def reaches(o):
        other = q + o
        apart = lax.div(other + 8, GROUP) - lax.div(q + 8, GROUP)
        return (other >= 0) & (other < planes) & (apart <= 1) & (apart >= -1)

    def remote(src, dst, ss, rs, device):
        return pltpu.make_async_remote_copy(
            src_ref=src, dst_ref=dst, send_sem=ss, recv_sem=rs,
            device_id=(device,), device_id_type=MESH,
        )

    def go(index, src, dst, device):
        return remote(src, dst, send.at[index], recv.at[index], device)

    own_copies = [
        pltpu.make_async_copy(
            probes.at[:, :, pl.ds(k * wide, wide)],
            bufs[k].at[pl.ds(1 + core, leaves)],
            near_sem.at[k],
        )
        for k in range(chunks)
    ]
    near_copy = pltpu.make_async_copy(near, near_f, near_sem.at[chunks])
    plane_clusters = cluster_hbm.at[pl.ds(q * GROUP, GROUP)]
    small_copies = [
        pltpu.make_async_copy(a, b, small_sem.at[i])
        for i, (a, b) in enumerate((
            (basis_hbm, basis), (transfer_hbm, transfer), (cone_hbm, cone), (ctwo_hbm, ctwo),
            (pone_hbm, pone), (none_hbm, none), (ntwo_hbm, ntwo),
            (plane_clusters, cluster), (nlist_hbm, nlist),
        ))
    ]
    for copy in small_copies[:2] + own_copies + small_copies[2:]:
        copy.start()

    barrier = pltpu.get_barrier_semaphore()

    def greet(device):
        pl.semaphore_signal(barrier, inc=1, device_id=(device,), device_id_type=MESH)

    greet(mate)
    for s in (1, 2, 3):
        greet(chip(xor(c4, s)))
    maybe = [(has_beside, beside), (q > 0, me - plane_size), (q < planes - 1, me + plane_size)]
    maybe += [(reaches(o), me + o * plane_size) for o in offsets]
    expected = jnp.int32(4)
    for there, device in maybe:
        pl.when(there)(functools.partial(greet, device))
        expected = expected + jnp.where(there, 1, 0)
    pl.semaphore_wait(barrier, expected)

    def halo(k, which):
        cols = pl.ds(k * wide, wide)
        if which == 0:
            dst = bufs[k].at[pl.ds((1 - core) * 4, 1)]
            src, device = probes.at[pl.ds(core, 1), :, cols], beside
        elif which == 1:
            dst = lasts[k]
            src, device = probes.at[pl.ds(1 - core, 1), :, cols], beside
        else:
            dst = bufs[k].at[pl.ds(core * 3, leaves)]
            src, device = probes.at[:, :, cols], mate
        return remote(src, dst, halo_send.at[which, k], halo_recv.at[which, k], device)

    def piece(p):
        pl.when(has_beside)(halo(p // 2, p % 2).start)

    piece(0)
    piece(1)
    near_copy.start()

    for copy in small_copies[:2]:
        copy.wait()
    flat = [dot(transfer[l].T, basis[l]) for l in range(leaves)]
    lifts = [split(value) for value in flat]
    for l in range(leaves):
        lift[l] = flat[l].T
    for k in range(chunks):
        own_copies[k].wait()
        value = sum(
            dot_split(lifts[l], split(bufs[k][1 + core + l]))
            for l in range(leaves)
        )
        for g in range(per_chunk):
            part[k * per_chunk + g] = value[:, g * LANES:(g + 1) * LANES]
    halve = go(0, part.at[pl.ds((1 - core) * GROUP, GROUP)], half, mate)
    halve.start()

    for copy in small_copies[2:]:
        copy.wait()
    slot = core * GROUP + c4
    slots = cone.shape[0]
    for s in range(slots // 2):
        packed[slot, pl.ds(s * rank, rank), :] = jnp.concatenate(
            [cone[2 * s], cone[2 * s + 1]], axis=1
        )
    packed[slot, pl.ds(slots // 2 * rank, rank), :] = jnp.concatenate([ctwo[0], ctwo[0]], axis=1)
    mine = q * GROUP + c4
    ids = [
        jnp.where(core * slots + k < none[mine], pone[k], -1) for k in range(slots)
    ]
    ids.append(jnp.where(r < ntwo[q], ptwo[0], -1))
    row = lax.broadcasted_iota(jnp.int32, (8, LANES), 0)
    table = jnp.full((8, LANES), -1, jnp.int32)
    for k, value in enumerate(ids):
        table = jnp.where(row == k, value, table)
    id_row = slots // 2 * rank + rank
    packed[slot, pl.ds(id_row, 8), :] = table.astype(jnp.float32)
    bit_x, bit_y = lax.rem(c4, 2), lax.div(c4, 2)
    pack_x = go(6, packed.at[pl.ds(slot, 1)], packed.at[pl.ds(slot, 1)], chip(xor(c4, 1)))
    pair = core * GROUP + bit_y * 2
    pack_y = go(7, packed.at[pl.ds(pair, 2)], packed.at[pl.ds(pair, 2)], chip(xor(c4, 2)))
    quad = core * GROUP
    pack_c = go(8, packed.at[pl.ds(quad, 4)], packed.at[pl.ds(quad, 4)], mate)
    pack_x.start()
    halve.wait_recv()
    for t in range(GROUP):
        share[t] = part[core * GROUP + t] + half[t]
    spread = [
        go(s, share.at[xor(c4, s)], coef.at[GROUP + c4], chip(xor(c4, s))) for s in (1, 2, 3)
    ]
    for copy in spread:
        copy.start()
    coef[GROUP + c4] = share[c4]
    piece(2)
    halo(0, 2).start()
    pack_x.wait_recv()
    pack_y.start()

    def near_split(index, _):
        l, m = lax.div(index, near.shape[1]), lax.rem(index, near.shape[1])
        near_h[l, m], near_l[l, m] = split(near_f[l, m])
        return _

    near_copy.wait()
    lax.fori_loop(0, leaves * near.shape[1], near_split, 0)

    for copy in spread:
        copy.wait_recv()
    up = go(4, coef.at[pl.ds(GROUP, GROUP)], coef.at[pl.ds(0, GROUP)], me + plane_size)
    lower = go(5, coef.at[pl.ds(GROUP, GROUP)], coef.at[pl.ds(2 * GROUP, GROUP)], me - plane_size)
    pl.when(q < planes - 1)(up.start)
    pl.when(q > 0)(lower.start)
    own_two[...] = sum(
        dot(cluster[j].T, coef[GROUP + j]) for j in range(GROUP)
    )
    two_copies = []
    for i, o in enumerate(offsets):
        copy = go(13 + i, own_two, two.at[offsets.index(-o)], me + o * plane_size)
        two_copies.append((o, copy))
        pl.when(reaches(o))(copy.start)
    piece(3)
    piece(4)
    halo(1, 2).start()
    pack_y.wait_recv()
    pack_c.start()

    def own_near(l, _):
        at = pl.ds(pl.multiple_of(l * size, size), size)
        for k in range(chunks):
            x = bufs[k][1 + core + l]
            total[at, k * wide:(k + 1) * wide] = dot_split((near_h[l, 0], near_l[l, 0]), split(x))
        return _

    lax.fori_loop(0, leaves, own_near, 0)

    pl.when(q > 0)(up.wait_recv)
    pl.when(q < planes - 1)(lower.wait_recv)
    for o, copy in two_copies:
        pl.when(reaches(-o))(copy.wait_recv)
    pack_c.wait_recv()

    zero = jnp.zeros((rank, LANES), jnp.float32)

    def chosen(at, k, options):
        picked = zero
        label = packed[at, pl.ds(id_row + k, 1), :]
        for number, value in options:
            picked = jnp.where(label == number.astype(jnp.float32), value, picked)
        return picked

    far_two = zero
    for at in range(plane_size):
        options = [(q + o, two[i]) for i, o in enumerate(offsets)]
        far_two += dot(
            packed[at, pl.ds(slots // 2 * rank, rank), :][:, :rank], chosen(at, slots, options)
        )

    far_two_split = split(far_two)

    def cluster_far(j, _):
        value = dot_split(split(cluster[j]), far_two_split)
        options = [((q - 1) * GROUP + i, coef[i]) for i in range(3 * GROUP)]
        for k in range(2):
            at = k * GROUP + j
            for s in range(slots // 2):
                partner = jnp.concatenate(
                    [chosen(at, 2 * s, options), chosen(at, 2 * s + 1, options)], axis=0
                )
                value += dot(packed[at, pl.ds(s * rank, rank), :], partner)
        down[j] = value
        return _

    lax.fori_loop(0, GROUP, cluster_far, 0)
    mine_at = core * GROUP + c4
    back = [
        go(8 + s, down.at[xor(c4, s)], dn.at[mine_at], chip(xor(c4, s))) for s in (1, 2, 3)
    ]
    for copy in back:
        copy.start()
    piece(5)
    halo(2, 2).start()
    dn[mine_at] = down[c4]
    for copy in back:
        copy.wait_recv()
    join = go(12, dn.at[pl.ds(quad, 4)], dn.at[pl.ds(quad, 4)], mate)
    join.start()
    piece(6)
    for k in range(3, chunks):
        halo(k, 2).start()
    pl.when(has_beside)(halo(2, 1).wait_send)
    piece(7)
    join.wait_recv()

    def far_rows(l, _):
        at = pl.ds(pl.multiple_of(l * size, size), size)
        tall = split(lift[l])
        for k in range(chunks):
            value = jnp.concatenate(
                [dn[k * per_chunk + g] for g in range(per_chunk)], axis=1
            )
            total[at, k * wide:(k + 1) * wide] += dot_split(tall, split(value))
        return _

    lax.fori_loop(0, leaves, far_rows, 0)

    def other_near(k, l, reach):
        at = pl.ds(pl.multiple_of(l * size, size), size)
        value = total[at, k * wide:(k + 1) * wide]
        for m in range(1, near.shape[1]):
            index = nlist[l, m] - (me - 1) * leaves
            held = jnp.maximum(0, jnp.minimum(index - 1 + core, 4))
            x = bufs[k][held]
            if reach:
                x = jnp.where(index == 5 * core, lasts[k][0], x)
            value += dot_split((near_h[l, m], near_l[l, m]), split(x))
        total[at, k * wide:(k + 1) * wide] = value

    results = []
    for k in range(chunks):
        halo(k, 2).wait_recv()
        pl.when(has_beside)(halo(k, 0).wait_recv)
        other_near(k, 1 - core, False)
        pl.when(has_beside)(halo(k, 1).wait_recv)
        other_near(k, core, True)
        copy = pltpu.make_async_copy(
            total.at[:, pl.ds(k * wide, wide)],
            out.at[:, pl.ds(k * wide, wide)],
            near_sem.at[k],
        )
        copy.start()
        results.append(copy)

    for copy in [halve, pack_x, pack_y, pack_c, join] + spread + back:
        copy.wait_send()
    pl.when(q < planes - 1)(up.wait_send)
    pl.when(q > 0)(lower.wait_send)
    for o, copy in two_copies:
        pl.when(reaches(o))(copy.wait_send)
    for k in range(chunks):
        halo(k, 2).wait_send()
        pl.when(has_beside)(halo(k, 0).wait_send)
        if k != 2:
            pl.when(has_beside)(halo(k, 1).wait_send)
    for copy in results:
        copy.wait()


def body(devices, *args):
    probes, basis, near = args[0], args[1], args[10]
    slots = args[4].shape[0]
    leaves, size, rank = basis.shape
    rows, width = probes.shape
    planes = devices // (2 * GROUP)
    offsets = tuple(o for o in partner_offsets if abs(o) < planes)
    chunks = 4
    groups = width // LANES
    wide = width // chunks
    assert leaves == 2 and groups == 2 * GROUP and 2 * rank == LANES
    smem = pl.BlockSpec(memory_space=pltpu.SMEM)
    anywhere = pl.BlockSpec(memory_space=pltpu.HBM)
    f32, bf16 = jnp.float32, jnp.bfloat16
    small = lambda n: pltpu.VMEM((n, rank, LANES), f32)
    dma = pltpu.SemaphoreType.DMA
    flops = 2 * (near.size + 2 * basis.size) * width
    result = pl.pallas_call(
        functools.partial(kernel, devices, offsets),
        out_shape=jax.ShapeDtypeStruct((rows, width), f32),
        in_specs=[anywhere] * 8 + [smem] + [anywhere] * (len(args) - 9),
        out_specs=anywhere,
        scratch_shapes=[pltpu.VMEM((5, size, wide), f32)] * chunks
        + [pltpu.VMEM((1, size, wide), f32)] * chunks
        + [
            pltpu.VMEM((leaves, rank, size), f32),
            pltpu.VMEM(args[2].shape, f32),
            pltpu.VMEM((GROUP, rank, rank), f32),
            pltpu.VMEM(args[4].shape, f32),
            pltpu.SMEM(args[5].shape, jnp.int32),
            pltpu.SMEM(args[6].shape, jnp.int32),
            pltpu.VMEM(args[7].shape, f32),
            pltpu.SMEM(args[9].shape, jnp.int32),
            pltpu.SMEM(args[11].shape, jnp.int32),
            dma((9,)),
            pltpu.VMEM(near.shape, f32),
            pltpu.VMEM(near.shape, bf16),
            pltpu.VMEM(near.shape, bf16),
            pltpu.VMEM((rows, width), f32),
            small(groups),
            small(GROUP),
            small(GROUP),
            small(3 * GROUP),
            pltpu.VMEM((rank, LANES), f32),
            small(max(1, len(offsets))),
            pltpu.VMEM((2 * GROUP, (slots // 2 + 1) * rank + 8, LANES), f32),
            small(GROUP),
            small(groups),
            pltpu.VMEM((leaves, size, rank), f32),
            dma((13 + len(offsets),)),
            dma((13 + len(offsets),)),
            dma((3, chunks)),
            dma((3, chunks)),
            dma((chunks + 1,)),
        ],
        compiler_params=pltpu.CompilerParams(
            collective_id=0, has_side_effects=True, vmem_limit_bytes=64 * 1024 * 1024 - 64 * 1024
        ),
        cost_estimate=pl.CostEstimate(
            flops=3 * flops, bytes_accessed=4 * (near.size + 4 * probes.size), transcendentals=0
        ),
    )(probes.reshape(leaves, size, width), jnp.swapaxes(basis, 1, 2), *args[2:])
    return pl.pallas_call(
        hand_over,
        out_shape=jax.ShapeDtypeStruct((rows, width), f32),
        in_specs=[anywhere],
        out_specs=anywhere,
        scratch_shapes=[dma((8,))],
    )(result)


def hand_over(src, dst, sem):
    parts = sem.shape[0]
    rows = src.shape[0] // parts
    copies = [
        pltpu.make_async_copy(src.at[pl.ds(i * rows, rows)], dst.at[pl.ds(i * rows, rows)], sem.at[i])
        for i in range(parts)
    ]
    for copy in copies:
        copy.start()
    for copy in copies:
        copy.wait()


def solution(mesh):
    return jax.shard_map(
        functools.partial(body, mesh.shape["leaf"]),
        mesh=mesh,
        in_specs=(
            P("leaf", None),
            P("leaf", None, None),
            P("leaf", None, None),
            P(),
            P("leaf", None, None),
            P("leaf"),
            P(),
            P("leaf", None, None),
            P("leaf"),
            P(),
            P("leaf", None, None, None),
            P("leaf", None),
        ),
        out_specs=P("leaf", None),
        check_vma=False,
    )
```

```python
import functools

import jax
import jax.numpy as jnp
from jax import lax
from jax.experimental import pallas as pl
from jax.experimental.pallas import tpu as pltpu
from jax.sharding import PartitionSpec as P

MESH = pl.DeviceIdType.MESH
GROUP = 4
LANES = 128
partner_offsets = (-7, -6, -5, -4, -3, -2, 2, 3, 4, 5, 6, 7)


def split(x):
    high = x.astype(jnp.bfloat16)
    low = (x - high.astype(jnp.float32)).astype(jnp.bfloat16)
    return high, low


def dot_split(a, b):
    one = functools.partial(jnp.dot, preferred_element_type=jnp.float32)
    return one(a[0], b[0]) + (one(a[0], b[1]) + one(a[1], b[0]))


def dot(a, b):
    return dot_split(split(a), split(b))


def kernel(
    devices,
    offsets,
    probes,
    basis_hbm,
    transfer_hbm,
    cluster_hbm,
    cone_hbm,
    pone_hbm,
    none_hbm,
    ctwo_hbm,
    ptwo,
    ntwo_hbm,
    near,
    nlist_hbm,
    out,
    *scratch,
):
    chunks = len(scratch) - 29
    bufs = scratch[:chunks]
    (basis, transfer, cluster, cone, pone, none, ctwo, ntwo, nlist, small_sem,
     near_f, near_h, near_l, total, part, half, share, coef, own_two, two, packed, down, dn, lift,
     send, recv, halo_send, halo_recv, near_sem) = scratch[chunks:]
    leaves, rank, size = basis.shape
    wide = bufs[0].shape[2]
    per_chunk = wide // LANES
    me = lax.axis_index("leaf")
    plane_size = GROUP * 2
    planes = devices // plane_size
    q = lax.div(me, plane_size)
    r = lax.rem(me, plane_size)
    core = lax.rem(r, 2)
    c4 = lax.div(r, 2)
    mate = me + 1 - 2 * core
    beside = me - 1 + 2 * core
    has_beside = (beside >= 0) & (beside < devices)

    def chip(t):
        return q * plane_size + t * 2 + core

    def xor(value, bits):
        result = value
        for bit in (1, 2):
            if bits & bit:
                result = result + bit - 2 * bit * lax.rem(lax.div(value, bit), 2)
        return result

    def reaches(o):
        other = q + o
        apart = lax.div(other + 8, GROUP) - lax.div(q + 8, GROUP)
        return (other >= 0) & (other < planes) & (apart <= 1) & (apart >= -1)

    def remote(src, dst, ss, rs, device):
        return pltpu.make_async_remote_copy(
            src_ref=src, dst_ref=dst, send_sem=ss, recv_sem=rs,
            device_id=(device,), device_id_type=MESH,
        )

    def go(index, src, dst, device):
        return remote(src, dst, send.at[index], recv.at[index], device)

    own_copies = [
        pltpu.make_async_copy(
            probes.at[:, :, pl.ds(k * wide, wide)],
            bufs[k].at[pl.ds(leaves, leaves)],
            near_sem.at[k],
        )
        for k in range(chunks)
    ]
    near_copy = pltpu.make_async_copy(near, near_f, near_sem.at[chunks])
    plane_clusters = cluster_hbm.at[pl.ds(q * GROUP, GROUP)]
    small_copies = [
        pltpu.make_async_copy(a, b, small_sem.at[i])
        for i, (a, b) in enumerate((
            (basis_hbm, basis), (transfer_hbm, transfer), (cone_hbm, cone), (ctwo_hbm, ctwo),
            (pone_hbm, pone), (none_hbm, none), (ntwo_hbm, ntwo),
            (plane_clusters, cluster), (nlist_hbm, nlist),
        ))
    ]
    for copy in small_copies[:2] + own_copies + small_copies[2:]:
        copy.start()

    barrier = pltpu.get_barrier_semaphore()

    def greet(device):
        pl.semaphore_signal(barrier, inc=1, device_id=(device,), device_id_type=MESH)

    greet(mate)
    for s in (1, 2, 3):
        greet(chip(xor(c4, s)))
    maybe = [(has_beside, beside), (q > 0, me - plane_size), (q < planes - 1, me + plane_size)]
    maybe += [(reaches(o), me + o * plane_size) for o in offsets]
    expected = jnp.int32(4)
    for there, device in maybe:
        pl.when(there)(functools.partial(greet, device))
        expected = expected + jnp.where(there, 1, 0)
    pl.semaphore_wait(barrier, expected)

    def halo(k, far, l=0):
        if far:
            src = probes.at[pl.ds(l, 1), :, pl.ds(k * wide, wide)]
            dst = bufs[k].at[pl.ds((1 - core) * 2 * leaves + l, 1)]
            return remote(src, dst, halo_send.at[l, k], halo_recv.at[l, k], beside)
        src = probes.at[:, :, pl.ds(k * wide, wide)]
        dst = bufs[k].at[pl.ds(core * 2 * leaves, leaves)]
        return remote(src, dst, halo_send.at[leaves, k], halo_recv.at[leaves, k], mate)

    def piece(p):
        copy = halo(p // leaves, True, p % leaves)
        pl.when(has_beside)(copy.start)

    piece(0)
    piece(1)
    near_copy.start()

    for copy in small_copies[:2]:
        copy.wait()
    flat = [dot(transfer[l].T, basis[l]) for l in range(leaves)]
    lifts = [split(value) for value in flat]
    for l in range(leaves):
        lift[l] = flat[l].T
    for k in range(chunks):
        own_copies[k].wait()
        value = sum(
            dot_split(lifts[l], split(bufs[k][leaves + l]))
            for l in range(leaves)
        )
        for g in range(per_chunk):
            part[k * per_chunk + g] = value[:, g * LANES:(g + 1) * LANES]
    halve = go(0, part.at[pl.ds((1 - core) * GROUP, GROUP)], half, mate)
    halve.start()

    for copy in small_copies[2:]:
        copy.wait()
    slot = core * GROUP + c4
    slots = cone.shape[0]
    for s in range(slots // 2):
        packed[slot, pl.ds(s * rank, rank), :] = jnp.concatenate(
            [cone[2 * s], cone[2 * s + 1]], axis=1
        )
    packed[slot, pl.ds(slots // 2 * rank, rank), :] = jnp.concatenate([ctwo[0], ctwo[0]], axis=1)
    mine = q * GROUP + c4
    ids = [
        jnp.where(core * slots + k < none[mine], pone[k], -1) for k in range(slots)
    ]
    ids.append(jnp.where(r < ntwo[q], ptwo[0], -1))
    row = lax.broadcasted_iota(jnp.int32, (8, LANES), 0)
    table = jnp.full((8, LANES), -1, jnp.int32)
    for k, value in enumerate(ids):
        table = jnp.where(row == k, value, table)
    id_row = slots // 2 * rank + rank
    packed[slot, pl.ds(id_row, 8), :] = table.astype(jnp.float32)
    bit_x, bit_y = lax.rem(c4, 2), lax.div(c4, 2)
    pack_x = go(6, packed.at[pl.ds(slot, 1)], packed.at[pl.ds(slot, 1)], chip(xor(c4, 1)))
    pair = core * GROUP + bit_y * 2
    pack_y = go(7, packed.at[pl.ds(pair, 2)], packed.at[pl.ds(pair, 2)], chip(xor(c4, 2)))
    quad = core * GROUP
    pack_c = go(8, packed.at[pl.ds(quad, 4)], packed.at[pl.ds(quad, 4)], mate)
    pack_x.start()
    halve.wait_recv()
    for t in range(GROUP):
        share[t] = part[core * GROUP + t] + half[t]
    spread = [
        go(s, share.at[xor(c4, s)], coef.at[GROUP + c4], chip(xor(c4, s))) for s in (1, 2, 3)
    ]
    for copy in spread:
        copy.start()
    coef[GROUP + c4] = share[c4]
    piece(2)
    halo(0, False).start()
    pack_x.wait_recv()
    pack_y.start()

    def near_split(index, _):
        l, m = lax.div(index, near.shape[1]), lax.rem(index, near.shape[1])
        near_h[l, m], near_l[l, m] = split(near_f[l, m])
        return _

    near_copy.wait()
    lax.fori_loop(0, leaves * near.shape[1], near_split, 0)

    for copy in spread:
        copy.wait_recv()
    up = go(4, coef.at[pl.ds(GROUP, GROUP)], coef.at[pl.ds(0, GROUP)], me + plane_size)
    lower = go(5, coef.at[pl.ds(GROUP, GROUP)], coef.at[pl.ds(2 * GROUP, GROUP)], me - plane_size)
    pl.when(q < planes - 1)(up.start)
    pl.when(q > 0)(lower.start)
    own_two[...] = sum(
        dot(cluster[j].T, coef[GROUP + j]) for j in range(GROUP)
    )
    two_copies = []
    for i, o in enumerate(offsets):
        copy = go(13 + i, own_two, two.at[offsets.index(-o)], me + o * plane_size)
        two_copies.append((o, copy))
        pl.when(reaches(o))(copy.start)
    piece(3)
    piece(4)
    piece(5)
    halo(1, False).start()
    pack_y.wait_recv()
    pack_c.start()

    def own_near(l, _):
        at = pl.ds(pl.multiple_of(l * size, size), size)
        for k in range(chunks):
            x = bufs[k][leaves + l]
            total[at, k * wide:(k + 1) * wide] = dot_split((near_h[l, 0], near_l[l, 0]), split(x))
        return _

    lax.fori_loop(0, leaves, own_near, 0)

    pl.when(q > 0)(up.wait_recv)
    pl.when(q < planes - 1)(lower.wait_recv)
    for o, copy in two_copies:
        pl.when(reaches(-o))(copy.wait_recv)
    pack_c.wait_recv()

    zero = jnp.zeros((rank, LANES), jnp.float32)

    def chosen(at, k, options):
        picked = zero
        label = packed[at, pl.ds(id_row + k, 1), :]
        for number, value in options:
            picked = jnp.where(label == number.astype(jnp.float32), value, picked)
        return picked

    far_two = zero
    for at in range(plane_size):
        options = [(q + o, two[i]) for i, o in enumerate(offsets)]
        far_two += dot(
            packed[at, pl.ds(slots // 2 * rank, rank), :][:, :rank], chosen(at, slots, options)
        )

    far_two_split = split(far_two)

    def cluster_far(j, _):
        value = dot_split(split(cluster[j]), far_two_split)
        options = [((q - 1) * GROUP + i, coef[i]) for i in range(3 * GROUP)]
        for k in range(2):
            at = k * GROUP + j
            for s in range(slots // 2):
                partner = jnp.concatenate(
                    [chosen(at, 2 * s, options), chosen(at, 2 * s + 1, options)], axis=0
                )
                value += dot(packed[at, pl.ds(s * rank, rank), :], partner)
        down[j] = value
        return _

    lax.fori_loop(0, GROUP, cluster_far, 0)
    mine_at = core * GROUP + c4
    back = [
        go(8 + s, down.at[xor(c4, s)], dn.at[mine_at], chip(xor(c4, s))) for s in (1, 2, 3)
    ]
    for copy in back:
        copy.start()
    piece(6)
    halo(2, False).start()
    dn[mine_at] = down[c4]
    for copy in back:
        copy.wait_recv()
    join = go(12, dn.at[pl.ds(quad, 4)], dn.at[pl.ds(quad, 4)], mate)
    join.start()
    for p in range(7, chunks * leaves):
        piece(p)
    for k in range(3, chunks):
        halo(k, False).start()
    join.wait_recv()

    def far_rows(l, _):
        at = pl.ds(pl.multiple_of(l * size, size), size)
        tall = split(lift[l])
        for k in range(chunks):
            value = jnp.concatenate(
                [dn[k * per_chunk + g] for g in range(per_chunk)], axis=1
            )
            total[at, k * wide:(k + 1) * wide] += dot_split(tall, split(value))
        return _

    lax.fori_loop(0, leaves, far_rows, 0)

    results = []
    for k in range(chunks):
        halo(k, False).wait_recv()
        for l in range(leaves):
            pl.when(has_beside)(halo(k, True, l).wait_recv)

        def other_near(l, _, k=k):
            at = pl.ds(pl.multiple_of(l * size, size), size)
            value = total[at, k * wide:(k + 1) * wide]
            for m in range(1, near.shape[1]):
                index = nlist[l, m] - (me - 1) * leaves
                index = jnp.maximum(0, jnp.minimum(index, 3 * leaves - 1))
                value += dot_split((near_h[l, m], near_l[l, m]), split(bufs[k][index]))
            total[at, k * wide:(k + 1) * wide] = value
            return _

        lax.fori_loop(0, leaves, other_near, 0)
        copy = pltpu.make_async_copy(
            total.at[:, pl.ds(k * wide, wide)],
            out.at[:, pl.ds(k * wide, wide)],
            near_sem.at[k],
        )
        copy.start()
        results.append(copy)

    for copy in [halve, pack_x, pack_y, pack_c, join] + spread + back:
        copy.wait_send()
    pl.when(q < planes - 1)(up.wait_send)
    pl.when(q > 0)(lower.wait_send)
    for o, copy in two_copies:
        pl.when(reaches(o))(copy.wait_send)
    for k in range(chunks):
        halo(k, False).wait_send()
        for l in range(leaves):
            pl.when(has_beside)(halo(k, True, l).wait_send)
    for copy in results:
        copy.wait()


def body(devices, *args):
    probes, basis, near = args[0], args[1], args[10]
    slots = args[4].shape[0]
    leaves, size, rank = basis.shape
    rows, width = probes.shape
    planes = devices // (2 * GROUP)
    offsets = tuple(o for o in partner_offsets if abs(o) < planes)
    chunks = 4
    groups = width // LANES
    wide = width // chunks
    assert leaves == 2 and groups == 2 * GROUP and 2 * rank == LANES
    smem = pl.BlockSpec(memory_space=pltpu.SMEM)
    anywhere = pl.BlockSpec(memory_space=pltpu.HBM)
    f32, bf16 = jnp.float32, jnp.bfloat16
    small = lambda n: pltpu.VMEM((n, rank, LANES), f32)
    dma = pltpu.SemaphoreType.DMA
    flops = 2 * (near.size + 2 * basis.size) * width
    result = pl.pallas_call(
        functools.partial(kernel, devices, offsets),
        out_shape=jax.ShapeDtypeStruct((rows, width), f32),
        in_specs=[anywhere] * 8 + [smem] + [anywhere] * (len(args) - 9),
        out_specs=anywhere,
        scratch_shapes=[pltpu.VMEM((3 * leaves, size, wide), f32)] * chunks
        + [
            pltpu.VMEM((leaves, rank, size), f32),
            pltpu.VMEM(args[2].shape, f32),
            pltpu.VMEM((GROUP, rank, rank), f32),
            pltpu.VMEM(args[4].shape, f32),
            pltpu.SMEM(args[5].shape, jnp.int32),
            pltpu.SMEM(args[6].shape, jnp.int32),
            pltpu.VMEM(args[7].shape, f32),
            pltpu.SMEM(args[9].shape, jnp.int32),
            pltpu.SMEM(args[11].shape, jnp.int32),
            dma((9,)),
            pltpu.VMEM(near.shape, f32),
            pltpu.VMEM(near.shape, bf16),
            pltpu.VMEM(near.shape, bf16),
            pltpu.VMEM((rows, width), f32),
            small(groups),
            small(GROUP),
            small(GROUP),
            small(3 * GROUP),
            pltpu.VMEM((rank, LANES), f32),
            small(max(1, len(offsets))),
            pltpu.VMEM((2 * GROUP, (slots // 2 + 1) * rank + 8, LANES), f32),
            small(GROUP),
            small(groups),
            pltpu.VMEM((leaves, size, rank), f32),
            dma((13 + len(offsets),)),
            dma((13 + len(offsets),)),
            dma((leaves + 1, chunks)),
            dma((leaves + 1, chunks)),
            dma((chunks + 1,)),
        ],
        compiler_params=pltpu.CompilerParams(
            collective_id=0, has_side_effects=True, vmem_limit_bytes=64 * 1024 * 1024 - 64 * 1024
        ),
        cost_estimate=pl.CostEstimate(
            flops=3 * flops, bytes_accessed=4 * (near.size + 4 * probes.size), transcendentals=0
        ),
    )(probes.reshape(leaves, size, width), jnp.swapaxes(basis, 1, 2), *args[2:])
    return pl.pallas_call(
        hand_over,
        out_shape=jax.ShapeDtypeStruct((rows, width), f32),
        in_specs=[anywhere],
        out_specs=anywhere,
        scratch_shapes=[pltpu.VMEM((rows, width), f32), dma((8,)), dma((8,))],
        compiler_params=pltpu.CompilerParams(vmem_limit_bytes=32 * 1024 * 1024),
    )(result)


def hand_over(src, dst, held, arrived, left):
    parts = arrived.shape[0]
    rows = src.shape[0] // parts
    at = [pl.ds(i * rows, rows) for i in range(parts)]
    into = [
        pltpu.make_async_copy(src.at[at[i]], held.at[at[i]], arrived.at[i]) for i in range(parts)
    ]
    away = [pltpu.make_async_copy(held.at[at[i]], dst.at[at[i]], left.at[i]) for i in range(parts)]
    for copy in into:
        copy.start()
    for i in range(parts):
        into[i].wait()
        away[i].start()
    for copy in away:
        copy.wait()


def solution(mesh):
    return jax.shard_map(
        functools.partial(body, mesh.shape["leaf"]),
        mesh=mesh,
        in_specs=(
            P("leaf", None),
            P("leaf", None, None),
            P("leaf", None, None),
            P(),
            P("leaf", None, None),
            P("leaf"),
            P(),
            P("leaf", None, None),
            P("leaf"),
            P(),
            P("leaf", None, None, None),
            P("leaf", None),
        ),
        out_specs=P("leaf", None),
        check_vma=False,
    )
```

```python
import functools

import jax
import jax.numpy as jnp
from jax import lax
from jax.experimental import pallas as pl
from jax.experimental.pallas import tpu as pltpu
from jax.sharding import PartitionSpec as P

MESH = pl.DeviceIdType.MESH
GROUP = 4
LANES = 128
partner_offsets = (-7, -6, -5, -4, -3, -2, 2, 3, 4, 5, 6, 7)


def split(x):
    high = x.astype(jnp.bfloat16)
    low = (x - high.astype(jnp.float32)).astype(jnp.bfloat16)
    return high, low


def dot_split(a, b):
    one = functools.partial(jnp.dot, preferred_element_type=jnp.float32)
    return one(a[0], b[0]) + (one(a[0], b[1]) + one(a[1], b[0]))


def dot(a, b):
    return dot_split(split(a), split(b))


def kernel(
    devices,
    offsets,
    probes,
    basis_hbm,
    transfer_hbm,
    cluster_hbm,
    cone_hbm,
    pone_hbm,
    none_hbm,
    ctwo_hbm,
    ptwo,
    ntwo_hbm,
    near,
    nlist_hbm,
    out,
    *scratch,
):
    chunks = len(scratch) - 29
    bufs = scratch[:chunks]
    (basis, transfer, cluster, cone, pone, none, ctwo, ntwo, nlist, small_sem,
     near_f, near_h, near_l, total, part, half, share, coef, own_two, two, packed, down, dn, lift,
     send, recv, halo_send, halo_recv, near_sem) = scratch[chunks:]
    leaves, rank, size = basis.shape
    wide = bufs[0].shape[2]
    per_chunk = wide // LANES
    me = lax.axis_index("leaf")
    plane_size = GROUP * 2
    planes = devices // plane_size
    q = lax.div(me, plane_size)
    r = lax.rem(me, plane_size)
    core = lax.rem(r, 2)
    c4 = lax.div(r, 2)
    mate = me + 1 - 2 * core
    beside = me - 1 + 2 * core
    has_beside = (beside >= 0) & (beside < devices)

    def chip(t):
        return q * plane_size + t * 2 + core

    def xor(value, bits):
        result = value
        for bit in (1, 2):
            if bits & bit:
                result = result + bit - 2 * bit * lax.rem(lax.div(value, bit), 2)
        return result

    def reaches(o):
        other = q + o
        apart = lax.div(other + 8, GROUP) - lax.div(q + 8, GROUP)
        return (other >= 0) & (other < planes) & (apart <= 1) & (apart >= -1)

    def remote(src, dst, ss, rs, device):
        return pltpu.make_async_remote_copy(
            src_ref=src, dst_ref=dst, send_sem=ss, recv_sem=rs,
            device_id=(device,), device_id_type=MESH,
        )

    def go(index, src, dst, device):
        return remote(src, dst, send.at[index], recv.at[index], device)

    own_copies = [
        pltpu.make_async_copy(
            probes.at[:, :, pl.ds(k * wide, wide)],
            bufs[k].at[pl.ds(leaves, leaves)],
            near_sem.at[k],
        )
        for k in range(chunks)
    ]
    near_copy = pltpu.make_async_copy(near, near_f, near_sem.at[chunks])
    plane_clusters = cluster_hbm.at[pl.ds(q * GROUP, GROUP)]
    small_copies = [
        pltpu.make_async_copy(a, b, small_sem.at[i])
        for i, (a, b) in enumerate((
            (basis_hbm, basis), (transfer_hbm, transfer), (cone_hbm, cone), (ctwo_hbm, ctwo),
            (pone_hbm, pone), (none_hbm, none), (ntwo_hbm, ntwo),
            (plane_clusters, cluster), (nlist_hbm, nlist),
        ))
    ]
    for copy in small_copies[:2] + own_copies + small_copies[2:]:
        copy.start()

    barrier = pltpu.get_barrier_semaphore()

    def greet(device):
        pl.semaphore_signal(barrier, inc=1, device_id=(device,), device_id_type=MESH)

    greet(mate)
    for s in (1, 2, 3):
        greet(chip(xor(c4, s)))
    maybe = [(has_beside, beside), (q > 0, me - plane_size), (q < planes - 1, me + plane_size)]
    maybe += [(reaches(o), me + o * plane_size) for o in offsets]
    expected = jnp.int32(4)
    for there, device in maybe:
        pl.when(there)(functools.partial(greet, device))
        expected = expected + jnp.where(there, 1, 0)
    pl.semaphore_wait(barrier, expected)

    def halo(k, far, l=0):
        if far:
            src = probes.at[pl.ds(l, 1), :, pl.ds(k * wide, wide)]
            dst = bufs[k].at[pl.ds((1 - core) * 2 * leaves + l, 1)]
            return remote(src, dst, halo_send.at[l, k], halo_recv.at[l, k], beside)
        src = probes.at[:, :, pl.ds(k * wide, wide)]
        dst = bufs[k].at[pl.ds(core * 2 * leaves, leaves)]
        return remote(src, dst, halo_send.at[leaves, k], halo_recv.at[leaves, k], mate)

    def piece(p):
        copy = halo(p // leaves, True, p % leaves)
        pl.when(has_beside)(copy.start)

    piece(0)
    piece(1)
    near_copy.start()

    for copy in small_copies[:2]:
        copy.wait()
    flat = [dot(transfer[l].T, basis[l]) for l in range(leaves)]
    lifts = [split(value) for value in flat]
    for l in range(leaves):
        lift[l] = flat[l].T
    for k in range(chunks):
        own_copies[k].wait()
        value = sum(
            dot_split(lifts[l], split(bufs[k][leaves + l]))
            for l in range(leaves)
        )
        for g in range(per_chunk):
            part[k * per_chunk + g] = value[:, g * LANES:(g + 1) * LANES]
    halve = go(0, part.at[pl.ds((1 - core) * GROUP, GROUP)], half, mate)
    halve.start()

    for copy in small_copies[2:]:
        copy.wait()
    slot = core * GROUP + c4
    slots = cone.shape[0]
    for s in range(slots // 2):
        packed[slot, pl.ds(s * rank, rank), :] = jnp.concatenate(
            [cone[2 * s], cone[2 * s + 1]], axis=1
        )
    packed[slot, pl.ds(slots // 2 * rank, rank // 2), :] = jnp.concatenate(
        [ctwo[0, : rank // 2], ctwo[0, rank // 2 :]], axis=1
    )
    mine = q * GROUP + c4
    ids = [
        jnp.where(core * slots + k < none[mine], pone[k], -1) for k in range(slots)
    ]
    ids.append(jnp.where(r < ntwo[q], ptwo[0], -1))
    row = lax.broadcasted_iota(jnp.int32, (8, LANES), 0)
    table = jnp.full((8, LANES), -1, jnp.int32)
    for k, value in enumerate(ids):
        table = jnp.where(row == k, value, table)
    id_row = slots // 2 * rank + rank // 2
    packed[slot, pl.ds(id_row, 8), :] = table.astype(jnp.float32)
    bit_x, bit_y = lax.rem(c4, 2), lax.div(c4, 2)
    pack_x = go(6, packed.at[pl.ds(slot, 1)], packed.at[pl.ds(slot, 1)], chip(xor(c4, 1)))
    pair = core * GROUP + bit_y * 2
    pack_y = go(7, packed.at[pl.ds(pair, 2)], packed.at[pl.ds(pair, 2)], chip(xor(c4, 2)))
    quad = core * GROUP
    pack_c = go(8, packed.at[pl.ds(quad, 4)], packed.at[pl.ds(quad, 4)], mate)
    pack_x.start()
    halve.wait_recv()
    for t in range(GROUP):
        share[t] = part[core * GROUP + t] + half[t]
    spread = [
        go(s, share.at[xor(c4, s)], coef.at[GROUP + c4], chip(xor(c4, s))) for s in (1, 2, 3)
    ]
    for copy in spread:
        copy.start()
    coef[GROUP + c4] = share[c4]
    piece(2)
    halo(0, False).start()
    pack_x.wait_recv()
    pack_y.start()

    def near_split(index, _):
        l, m = lax.div(index, near.shape[1]), lax.rem(index, near.shape[1])
        near_h[l, m], near_l[l, m] = split(near_f[l, m])
        return _

    near_copy.wait()
    lax.fori_loop(0, leaves * near.shape[1], near_split, 0)

    for copy in spread:
        copy.wait_recv()
    up = go(4, coef.at[pl.ds(GROUP, GROUP)], coef.at[pl.ds(0, GROUP)], me + plane_size)
    lower = go(5, coef.at[pl.ds(GROUP, GROUP)], coef.at[pl.ds(2 * GROUP, GROUP)], me - plane_size)
    pl.when(q < planes - 1)(up.start)
    pl.when(q > 0)(lower.start)
    own_two[...] = sum(
        dot(cluster[j].T, coef[GROUP + j]) for j in range(GROUP)
    )
    two_copies = []
    for i, o in enumerate(offsets):
        copy = go(13 + i, own_two, two.at[offsets.index(-o)], me + o * plane_size)
        two_copies.append((o, copy))
        pl.when(reaches(o))(copy.start)
    piece(3)
    piece(4)
    halo(1, False).start()
    pack_y.wait_recv()
    pack_c.start()

    def own_near(l, _):
        at = pl.ds(pl.multiple_of(l * size, size), size)
        for k in range(chunks):
            x = bufs[k][leaves + l]
            total[at, k * wide:(k + 1) * wide] = dot_split((near_h[l, 0], near_l[l, 0]), split(x))
        return _

    lax.fori_loop(0, leaves, own_near, 0)

    pl.when(q > 0)(up.wait_recv)
    pl.when(q < planes - 1)(lower.wait_recv)
    for o, copy in two_copies:
        pl.when(reaches(-o))(copy.wait_recv)
    pack_c.wait_recv()

    zero = jnp.zeros((rank, LANES), jnp.float32)

    def chosen(at, k, options):
        picked = zero
        label = packed[at, pl.ds(id_row + k, 1), :]
        for number, value in options:
            picked = jnp.where(label == number.astype(jnp.float32), value, picked)
        return picked

    far_two = zero
    for at in range(plane_size):
        options = [(q + o, two[i]) for i, o in enumerate(offsets)]
        folded = packed[at, pl.ds(slots // 2 * rank, rank // 2), :]
        block = jnp.concatenate([folded[:, :rank], folded[:, rank:]], axis=0)
        far_two += dot(block, chosen(at, slots, options))

    far_two_split = split(far_two)

    def cluster_far(j, _):
        value = dot_split(split(cluster[j]), far_two_split)
        options = [((q - 1) * GROUP + i, coef[i]) for i in range(3 * GROUP)]
        for k in range(2):
            at = k * GROUP + j
            for s in range(slots // 2):
                partner = jnp.concatenate(
                    [chosen(at, 2 * s, options), chosen(at, 2 * s + 1, options)], axis=0
                )
                value += dot(packed[at, pl.ds(s * rank, rank), :], partner)
        down[j] = value
        return _

    lax.fori_loop(0, GROUP, cluster_far, 0)
    mine_at = core * GROUP + c4
    back = [
        go(8 + s, down.at[xor(c4, s)], dn.at[mine_at], chip(xor(c4, s))) for s in (1, 2, 3)
    ]
    for copy in back:
        copy.start()
    piece(5)
    halo(2, False).start()
    dn[mine_at] = down[c4]
    for copy in back:
        copy.wait_recv()
    join = go(12, dn.at[pl.ds(quad, 4)], dn.at[pl.ds(quad, 4)], mate)
    join.start()
    for p in range(6, chunks * leaves):
        piece(p)
    for k in range(3, chunks):
        halo(k, False).start()
    join.wait_recv()

    def far_rows(l, _):
        at = pl.ds(pl.multiple_of(l * size, size), size)
        tall = split(lift[l])
        for k in range(chunks):
            value = jnp.concatenate(
                [dn[k * per_chunk + g] for g in range(per_chunk)], axis=1
            )
            total[at, k * wide:(k + 1) * wide] += dot_split(tall, split(value))
        return _

    lax.fori_loop(0, leaves, far_rows, 0)

    results = []
    for k in range(chunks):
        halo(k, False).wait_recv()
        for l in range(leaves):
            pl.when(has_beside)(halo(k, True, l).wait_recv)

        def other_near(l, _, k=k):
            at = pl.ds(pl.multiple_of(l * size, size), size)
            value = total[at, k * wide:(k + 1) * wide]
            for m in range(1, near.shape[1]):
                index = nlist[l, m] - (me - 1) * leaves
                index = jnp.maximum(0, jnp.minimum(index, 3 * leaves - 1))
                value += dot_split((near_h[l, m], near_l[l, m]), split(bufs[k][index]))
            total[at, k * wide:(k + 1) * wide] = value
            return _

        lax.fori_loop(0, leaves, other_near, 0)
        copy = pltpu.make_async_copy(
            total.at[:, pl.ds(k * wide, wide)],
            out.at[:, pl.ds(k * wide, wide)],
            near_sem.at[k],
        )
        copy.start()
        results.append(copy)

    for copy in [halve, pack_x, pack_y, pack_c, join] + spread + back:
        copy.wait_send()
    pl.when(q < planes - 1)(up.wait_send)
    pl.when(q > 0)(lower.wait_send)
    for o, copy in two_copies:
        pl.when(reaches(o))(copy.wait_send)
    for k in range(chunks):
        halo(k, False).wait_send()
        for l in range(leaves):
            pl.when(has_beside)(halo(k, True, l).wait_send)
    for copy in results:
        copy.wait()


def body(devices, *args):
    probes, basis, near = args[0], args[1], args[10]
    slots = args[4].shape[0]
    leaves, size, rank = basis.shape
    rows, width = probes.shape
    planes = devices // (2 * GROUP)
    offsets = tuple(o for o in partner_offsets if abs(o) < planes)
    chunks = 4
    groups = width // LANES
    wide = width // chunks
    assert leaves == 2 and groups == 2 * GROUP and 2 * rank == LANES
    smem = pl.BlockSpec(memory_space=pltpu.SMEM)
    anywhere = pl.BlockSpec(memory_space=pltpu.HBM)
    f32, bf16 = jnp.float32, jnp.bfloat16
    small = lambda n: pltpu.VMEM((n, rank, LANES), f32)
    dma = pltpu.SemaphoreType.DMA
    flops = 2 * (near.size + 2 * basis.size) * width
    result = pl.pallas_call(
        functools.partial(kernel, devices, offsets),
        out_shape=jax.ShapeDtypeStruct((rows, width), f32),
        in_specs=[anywhere] * 8 + [smem] + [anywhere] * (len(args) - 9),
        out_specs=anywhere,
        scratch_shapes=[pltpu.VMEM((3 * leaves, size, wide), f32)] * chunks
        + [
            pltpu.VMEM((leaves, rank, size), f32),
            pltpu.VMEM(args[2].shape, f32),
            pltpu.VMEM((GROUP, rank, rank), f32),
            pltpu.VMEM(args[4].shape, f32),
            pltpu.SMEM(args[5].shape, jnp.int32),
            pltpu.SMEM(args[6].shape, jnp.int32),
            pltpu.VMEM(args[7].shape, f32),
            pltpu.SMEM(args[9].shape, jnp.int32),
            pltpu.SMEM(args[11].shape, jnp.int32),
            dma((9,)),
            pltpu.VMEM(near.shape, f32),
            pltpu.VMEM(near.shape, bf16),
            pltpu.VMEM(near.shape, bf16),
            pltpu.VMEM((rows, width), f32),
            small(groups),
            small(GROUP),
            small(GROUP),
            small(3 * GROUP),
            pltpu.VMEM((rank, LANES), f32),
            small(max(1, len(offsets))),
            pltpu.VMEM((2 * GROUP, slots // 2 * rank + rank // 2 + 8, LANES), f32),
            small(GROUP),
            small(groups),
            pltpu.VMEM((leaves, size, rank), f32),
            dma((13 + len(offsets),)),
            dma((13 + len(offsets),)),
            dma((leaves + 1, chunks)),
            dma((leaves + 1, chunks)),
            dma((chunks + 1,)),
        ],
        compiler_params=pltpu.CompilerParams(
            collective_id=0, has_side_effects=True, vmem_limit_bytes=64 * 1024 * 1024 - 64 * 1024
        ),
        cost_estimate=pl.CostEstimate(
            flops=3 * flops, bytes_accessed=4 * (near.size + 4 * probes.size), transcendentals=0
        ),
    )(probes.reshape(leaves, size, width), jnp.swapaxes(basis, 1, 2), *args[2:])
    return pl.pallas_call(
        hand_over,
        out_shape=jax.ShapeDtypeStruct((rows, width), f32),
        in_specs=[anywhere],
        out_specs=anywhere,
        scratch_shapes=[pltpu.VMEM((rows, width), f32), dma((16,)), dma((16,))],
        compiler_params=pltpu.CompilerParams(vmem_limit_bytes=64 * 1024 * 1024 - 64 * 1024),
    )(result)


def hand_over(src, dst, held, arrived, left):
    parts = arrived.shape[0]
    rows = src.shape[0] // parts
    at = [pl.ds(i * rows, rows) for i in range(parts)]
    into = [
        pltpu.make_async_copy(src.at[at[i]], held.at[at[i]], arrived.at[i]) for i in range(parts)
    ]
    away = [pltpu.make_async_copy(held.at[at[i]], dst.at[at[i]], left.at[i]) for i in range(parts)]
    for copy in into:
        copy.start()
    for i in range(parts):
        into[i].wait()
        away[i].start()
    for copy in away:
        copy.wait()


def solution(mesh):
    return jax.shard_map(
        functools.partial(body, mesh.shape["leaf"]),
        mesh=mesh,
        in_specs=(
            P("leaf", None),
            P("leaf", None, None),
            P("leaf", None, None),
            P(),
            P("leaf", None, None),
            P("leaf"),
            P(),
            P("leaf", None, None),
            P("leaf"),
            P(),
            P("leaf", None, None, None),
            P("leaf", None),
        ),
        out_specs=P("leaf", None),
        check_vma=False,
    )
```

```python
import functools

import jax
import jax.numpy as jnp
from jax import lax
from jax.experimental import pallas as pl
from jax.experimental.pallas import tpu as pltpu
from jax.sharding import PartitionSpec as P

MESH = pl.DeviceIdType.MESH
GROUP = 4
LANES = 128
partner_offsets = (-7, -6, -5, -4, -3, -2, 2, 3, 4, 5, 6, 7)


def split(x):
    high = x.astype(jnp.bfloat16)
    low = (x - high.astype(jnp.float32)).astype(jnp.bfloat16)
    return high, low


def dot_split(a, b):
    one = functools.partial(jnp.dot, preferred_element_type=jnp.float32)
    return one(a[0], b[0]) + (one(a[0], b[1]) + one(a[1], b[0]))


def dot(a, b):
    return dot_split(split(a), split(b))


def kernel(
    devices,
    offsets,
    probes,
    basis_hbm,
    transfer_hbm,
    cluster_hbm,
    cone_hbm,
    pone_hbm,
    none_hbm,
    ctwo_hbm,
    ptwo,
    ntwo_hbm,
    near,
    nlist_hbm,
    out,
    *scratch,
):
    chunks = len(scratch) - 29
    bufs = scratch[:chunks]
    (basis, transfer, cluster, cone, pone, none, ctwo, ntwo, nlist, small_sem,
     near_f, near_h, near_l, total, part, half, share, coef, own_two, two, packed, down, dn, lift,
     send, recv, halo_send, halo_recv, near_sem) = scratch[chunks:]
    leaves, rank, size = basis.shape
    wide = bufs[0].shape[2]
    per_chunk = wide // LANES
    me = lax.axis_index("leaf")
    plane_size = GROUP * 2
    planes = devices // plane_size
    q = lax.div(me, plane_size)
    r = lax.rem(me, plane_size)
    core = lax.rem(r, 2)
    c4 = lax.div(r, 2)
    mate = me + 1 - 2 * core
    beside = me - 1 + 2 * core
    has_beside = (beside >= 0) & (beside < devices)

    def chip(t):
        return q * plane_size + t * 2 + core

    def xor(value, bits):
        result = value
        for bit in (1, 2):
            if bits & bit:
                result = result + bit - 2 * bit * lax.rem(lax.div(value, bit), 2)
        return result

    def reaches(o):
        other = q + o
        apart = lax.div(other + 8, GROUP) - lax.div(q + 8, GROUP)
        return (other >= 0) & (other < planes) & (apart <= 1) & (apart >= -1)

    def remote(src, dst, ss, rs, device):
        return pltpu.make_async_remote_copy(
            src_ref=src, dst_ref=dst, send_sem=ss, recv_sem=rs,
            device_id=(device,), device_id_type=MESH,
        )

    def go(index, src, dst, device):
        return remote(src, dst, send.at[index], recv.at[index], device)

    own_copies = [
        pltpu.make_async_copy(
            probes.at[:, :, pl.ds(k * wide, wide)],
            bufs[k].at[pl.ds(leaves, leaves)],
            near_sem.at[k],
        )
        for k in range(chunks)
    ]
    near_copy = pltpu.make_async_copy(near, near_f, near_sem.at[chunks])
    plane_clusters = cluster_hbm.at[pl.ds(q * GROUP, GROUP)]
    small_copies = [
        pltpu.make_async_copy(a, b, small_sem.at[i])
        for i, (a, b) in enumerate((
            (basis_hbm, basis), (transfer_hbm, transfer), (cone_hbm, cone), (ctwo_hbm, ctwo),
            (pone_hbm, pone), (none_hbm, none), (ntwo_hbm, ntwo),
            (plane_clusters, cluster), (nlist_hbm, nlist),
        ))
    ]
    for copy in small_copies[:2] + own_copies + small_copies[2:]:
        copy.start()

    barrier = pltpu.get_barrier_semaphore()

    def greet(device):
        pl.semaphore_signal(barrier, inc=1, device_id=(device,), device_id_type=MESH)

    greet(mate)
    for s in (1, 2, 3):
        greet(chip(xor(c4, s)))
    maybe = [(has_beside, beside), (q > 0, me - plane_size), (q < planes - 1, me + plane_size)]
    maybe += [(reaches(o), me + o * plane_size) for o in offsets]
    expected = jnp.int32(4)
    for there, device in maybe:
        pl.when(there)(functools.partial(greet, device))
        expected = expected + jnp.where(there, 1, 0)
    pl.semaphore_wait(barrier, expected)

    def halo(k, far, l=0):
        if far:
            src = probes.at[pl.ds(l, 1), :, pl.ds(k * wide, wide)]
            dst = bufs[k].at[pl.ds((1 - core) * 2 * leaves + l, 1)]
            return remote(src, dst, halo_send.at[l, k], halo_recv.at[l, k], beside)
        src = probes.at[:, :, pl.ds(k * wide, wide)]
        dst = bufs[k].at[pl.ds(core * 2 * leaves, leaves)]
        return remote(src, dst, halo_send.at[leaves, k], halo_recv.at[leaves, k], mate)

    def piece(p):
        copy = halo(p // leaves, True, p % leaves)
        pl.when(has_beside)(copy.start)

    piece(0)
    piece(1)
    near_copy.start()

    for copy in small_copies[:2]:
        copy.wait()
    flat = [dot(transfer[l].T, basis[l]) for l in range(leaves)]
    lifts = [split(value) for value in flat]
    for l in range(leaves):
        lift[l] = flat[l].T
    for k in range(chunks):
        own_copies[k].wait()
        value = sum(
            dot_split(lifts[l], split(bufs[k][leaves + l]))
            for l in range(leaves)
        )
        for g in range(per_chunk):
            part[k * per_chunk + g] = value[:, g * LANES:(g + 1) * LANES]
    halve = go(0, part.at[pl.ds((1 - core) * GROUP, GROUP)], half, mate)
    halve.start()

    for copy in small_copies[2:]:
        copy.wait()
    slot = core * GROUP + c4
    slots = cone.shape[0]
    for s in range(slots // 2):
        packed[slot, pl.ds(s * rank, rank), :] = jnp.concatenate(
            [cone[2 * s], cone[2 * s + 1]], axis=1
        )
    packed[slot, pl.ds(slots // 2 * rank, rank // 2), :] = jnp.concatenate(
        [ctwo[0, : rank // 2], ctwo[0, rank // 2 :]], axis=1
    )
    mine = q * GROUP + c4
    ids = [
        jnp.where(core * slots + k < none[mine], pone[k], -1) for k in range(slots)
    ]
    ids.append(jnp.where(r < ntwo[q], ptwo[0], -1))
    row = lax.broadcasted_iota(jnp.int32, (8, LANES), 0)
    table = jnp.full((8, LANES), -1, jnp.int32)
    for k, value in enumerate(ids):
        table = jnp.where(row == k, value, table)
    id_row = slots // 2 * rank + rank // 2
    packed[slot, pl.ds(id_row, 8), :] = table.astype(jnp.float32)
    bit_x, bit_y = lax.rem(c4, 2), lax.div(c4, 2)
    pack_x = go(6, packed.at[pl.ds(slot, 1)], packed.at[pl.ds(slot, 1)], chip(xor(c4, 1)))
    pair = core * GROUP + bit_y * 2
    pack_y = go(7, packed.at[pl.ds(pair, 2)], packed.at[pl.ds(pair, 2)], chip(xor(c4, 2)))
    quad = core * GROUP
    pack_c = go(8, packed.at[pl.ds(quad, 4)], packed.at[pl.ds(quad, 4)], mate)
    pack_x.start()
    halve.wait_recv()
    for t in range(GROUP):
        share[t] = part[core * GROUP + t] + half[t]
    spread = [
        go(s, share.at[xor(c4, s)], coef.at[GROUP + c4], chip(xor(c4, s))) for s in (1, 2, 3)
    ]
    for copy in spread:
        copy.start()
    coef[GROUP + c4] = share[c4]
    piece(2)
    halo(0, False).start()
    pack_x.wait_recv()
    pack_y.start()

    def near_split(index, _):
        l, m = lax.div(index, near.shape[1]), lax.rem(index, near.shape[1])
        near_h[l, m], near_l[l, m] = split(near_f[l, m])
        return _

    near_copy.wait()
    lax.fori_loop(0, leaves * near.shape[1], near_split, 0)

    for copy in spread:
        copy.wait_recv()
    up = go(4, coef.at[pl.ds(GROUP, GROUP)], coef.at[pl.ds(0, GROUP)], me + plane_size)
    lower = go(5, coef.at[pl.ds(GROUP, GROUP)], coef.at[pl.ds(2 * GROUP, GROUP)], me - plane_size)
    pl.when(q < planes - 1)(up.start)
    pl.when(q > 0)(lower.start)
    own_two[...] = sum(
        dot(cluster[j].T, coef[GROUP + j]) for j in range(GROUP)
    )
    two_copies = []
    for i, o in enumerate(offsets):
        copy = go(13 + i, own_two, two.at[offsets.index(-o)], me + o * plane_size)
        two_copies.append((o, copy))
        pl.when(reaches(o))(copy.start)
    piece(3)
    piece(4)
    halo(1, False).start()
    pack_y.wait_recv()
    pack_c.start()

    def own_near(l, _):
        at = pl.ds(pl.multiple_of(l * size, size), size)
        for k in range(chunks):
            x = bufs[k][leaves + l]
            total[at, k * wide:(k + 1) * wide] = dot_split((near_h[l, 0], near_l[l, 0]), split(x))
        return _

    lax.fori_loop(0, leaves, own_near, 0)

    pl.when(q > 0)(up.wait_recv)
    pl.when(q < planes - 1)(lower.wait_recv)
    for o, copy in two_copies:
        pl.when(reaches(-o))(copy.wait_recv)
    pack_c.wait_recv()

    zero = jnp.zeros((rank, LANES), jnp.float32)

    def chosen(at, k, options):
        picked = zero
        label = packed[at, pl.ds(id_row + k, 1), :]
        for number, value in options:
            picked = jnp.where(label == number.astype(jnp.float32), value, picked)
        return picked

    far_two = zero
    for at in range(plane_size):
        options = [(q + o, two[i]) for i, o in enumerate(offsets)]
        folded = packed[at, pl.ds(slots // 2 * rank, rank // 2), :]
        block = jnp.concatenate([folded[:, :rank], folded[:, rank:]], axis=0)
        far_two += dot(block, chosen(at, slots, options))

    far_two_split = split(far_two)

    def cluster_far(j, _):
        value = dot_split(split(cluster[j]), far_two_split)
        options = [((q - 1) * GROUP + i, coef[i]) for i in range(3 * GROUP)]
        for k in range(2):
            at = k * GROUP + j
            for s in range(slots // 2):
                partner = jnp.concatenate(
                    [chosen(at, 2 * s, options), chosen(at, 2 * s + 1, options)], axis=0
                )
                value += dot(packed[at, pl.ds(s * rank, rank), :], partner)
        down[j] = value
        return _

    lax.fori_loop(0, GROUP, cluster_far, 0)
    mine_at = core * GROUP + c4
    back = [
        go(8 + s, down.at[xor(c4, s)], dn.at[mine_at], chip(xor(c4, s))) for s in (1, 2, 3)
    ]
    for copy in back:
        copy.start()
    piece(5)
    halo(2, False).start()
    dn[mine_at] = down[c4]
    for copy in back:
        copy.wait_recv()
    join = go(12, dn.at[pl.ds(quad, 4)], dn.at[pl.ds(quad, 4)], mate)
    join.start()
    for p in range(6, chunks * leaves):
        piece(p)
    for k in range(3, chunks):
        halo(k, False).start()
    join.wait_recv()

    def far_rows(l, _):
        at = pl.ds(pl.multiple_of(l * size, size), size)
        tall = split(lift[l])
        for k in range(chunks):
            value = jnp.concatenate(
                [dn[k * per_chunk + g] for g in range(per_chunk)], axis=1
            )
            total[at, k * wide:(k + 1) * wide] += dot_split(tall, split(value))
        return _

    lax.fori_loop(0, leaves, far_rows, 0)

    results = []
    for k in range(chunks):
        halo(k, False).wait_recv()
        for l in range(leaves):
            pl.when(has_beside)(halo(k, True, l).wait_recv)

        def other_near(l, _, k=k):
            at = pl.ds(pl.multiple_of(l * size, size), size)
            value = total[at, k * wide:(k + 1) * wide]
            for m in range(1, near.shape[1]):
                index = nlist[l, m] - (me - 1) * leaves
                index = jnp.maximum(0, jnp.minimum(index, 3 * leaves - 1))
                value += dot_split((near_h[l, m], near_l[l, m]), split(bufs[k][index]))
            total[at, k * wide:(k + 1) * wide] = value
            return _

        groups = leaves if k == chunks - 1 else 1
        tall = leaves // groups
        for l in range(groups):
            lax.fori_loop(l * tall, (l + 1) * tall, other_near, 0)
            at = pl.ds(l * tall * size, tall * size)
            copy = pltpu.make_async_copy(
                total.at[at, pl.ds(k * wide, wide)],
                out.at[at, pl.ds(k * wide, wide)],
                near_sem.at[k + l],
            )
            copy.start()
            results.append(copy)

    for copy in [halve, pack_x, pack_y, pack_c, join] + spread + back:
        copy.wait_send()
    pl.when(q < planes - 1)(up.wait_send)
    pl.when(q > 0)(lower.wait_send)
    for o, copy in two_copies:
        pl.when(reaches(o))(copy.wait_send)
    for k in range(chunks):
        halo(k, False).wait_send()
        for l in range(leaves):
            pl.when(has_beside)(halo(k, True, l).wait_send)
    for copy in results:
        copy.wait()


def body(devices, *args):
    probes, basis, near = args[0], args[1], args[10]
    slots = args[4].shape[0]
    leaves, size, rank = basis.shape
    rows, width = probes.shape
    planes = devices // (2 * GROUP)
    offsets = tuple(o for o in partner_offsets if abs(o) < planes)
    chunks = 4
    groups = width // LANES
    wide = width // chunks
    assert leaves == 2 and groups == 2 * GROUP and 2 * rank == LANES
    smem = pl.BlockSpec(memory_space=pltpu.SMEM)
    anywhere = pl.BlockSpec(memory_space=pltpu.HBM)
    f32, bf16 = jnp.float32, jnp.bfloat16
    small = lambda n: pltpu.VMEM((n, rank, LANES), f32)
    dma = pltpu.SemaphoreType.DMA
    flops = 2 * (near.size + 2 * basis.size) * width
    result = pl.pallas_call(
        functools.partial(kernel, devices, offsets),
        out_shape=jax.ShapeDtypeStruct((rows, width), f32),
        in_specs=[anywhere] * 8 + [smem] + [anywhere] * (len(args) - 9),
        out_specs=anywhere,
        scratch_shapes=[pltpu.VMEM((3 * leaves, size, wide), f32)] * chunks
        + [
            pltpu.VMEM((leaves, rank, size), f32),
            pltpu.VMEM(args[2].shape, f32),
            pltpu.VMEM((GROUP, rank, rank), f32),
            pltpu.VMEM(args[4].shape, f32),
            pltpu.SMEM(args[5].shape, jnp.int32),
            pltpu.SMEM(args[6].shape, jnp.int32),
            pltpu.VMEM(args[7].shape, f32),
            pltpu.SMEM(args[9].shape, jnp.int32),
            pltpu.SMEM(args[11].shape, jnp.int32),
            dma((9,)),
            pltpu.VMEM(near.shape, f32),
            pltpu.VMEM(near.shape, bf16),
            pltpu.VMEM(near.shape, bf16),
            pltpu.VMEM((rows, width), f32),
            small(groups),
            small(GROUP),
            small(GROUP),
            small(3 * GROUP),
            pltpu.VMEM((rank, LANES), f32),
            small(max(1, len(offsets))),
            pltpu.VMEM((2 * GROUP, slots // 2 * rank + rank // 2 + 8, LANES), f32),
            small(GROUP),
            small(groups),
            pltpu.VMEM((leaves, size, rank), f32),
            dma((13 + len(offsets),)),
            dma((13 + len(offsets),)),
            dma((leaves + 1, chunks)),
            dma((leaves + 1, chunks)),
            dma((chunks + 1,)),
        ],
        compiler_params=pltpu.CompilerParams(
            collective_id=0, has_side_effects=True, vmem_limit_bytes=64 * 1024 * 1024 - 64 * 1024
        ),
        cost_estimate=pl.CostEstimate(
            flops=3 * flops, bytes_accessed=4 * (near.size + 4 * probes.size), transcendentals=0
        ),
    )(probes.reshape(leaves, size, width), jnp.swapaxes(basis, 1, 2), *args[2:])
    return pl.pallas_call(
        hand_over,
        out_shape=jax.ShapeDtypeStruct((rows, width), f32),
        in_specs=[anywhere],
        out_specs=anywhere,
        scratch_shapes=[pltpu.VMEM((rows, width), f32), dma((16,)), dma((16,))],
        compiler_params=pltpu.CompilerParams(vmem_limit_bytes=64 * 1024 * 1024 - 64 * 1024),
    )(result)


def hand_over(src, dst, held, arrived, left):
    parts = arrived.shape[0]
    rows = src.shape[0] // parts
    at = [pl.ds(i * rows, rows) for i in range(parts)]
    into = [
        pltpu.make_async_copy(src.at[at[i]], held.at[at[i]], arrived.at[i]) for i in range(parts)
    ]
    away = [pltpu.make_async_copy(held.at[at[i]], dst.at[at[i]], left.at[i]) for i in range(parts)]
    for copy in into:
        copy.start()
    for i in range(parts):
        into[i].wait()
        away[i].start()
    for copy in away:
        copy.wait()


def solution(mesh):
    return jax.shard_map(
        functools.partial(body, mesh.shape["leaf"]),
        mesh=mesh,
        in_specs=(
            P("leaf", None),
            P("leaf", None, None),
            P("leaf", None, None),
            P(),
            P("leaf", None, None),
            P("leaf"),
            P(),
            P("leaf", None, None),
            P("leaf"),
            P(),
            P("leaf", None, None, None),
            P("leaf", None),
        ),
        out_specs=P("leaf", None),
        check_vma=False,
    )
```
